32 devices in a mesh: grp: 2 (over x), rp: 8 (over z, y), re: 2 (over core).
Axes of the slice: x: 2, y: 2, z: 4, core: 2. Of those that a mesh axis runs over, the one named last changes fastest.
Arguments:
- weights: bfloat16 [2, 256, 8, 48, 256], P(None, 'rp', 're'), may hold values from -0.125 to 0.125
- rp_vectors: int32 [3, 256], P(None, 'rp'), may hold values from -6 to 6, as said below
- re_vectors: int32 [3, 8], replicated, may hold values from -6 to 6, as said below
- q_points: int32 [3, 16], P(None, 'grp'), parts along dimension 1, may hold values from 0 to 47
- k_points: int32 [3, 4], P(None, 'grp'), parts along dimension 1, may hold values from 0 to 47
- eigvecs: float32 [16, 2, 48, 48], P(('grp', 'rp')), parts along dimension 0, may hold values from -0.625 to 0.625
Outputs:
- bloch_out: bfloat16 [16, 2, 2, 48, 256], P(('grp', 'rp'), None, 're'), parts along dimension 0
The draws below stay inside these ranges and needn't reach their ends.
There are 2 independent parts, one for each index of `grp`. The reference program is written for one: setup_inputs(seed, part) draws one part's arguments, and reference() takes and returns one part's arrays. A program takes and returns all parts, laid end to end along the dimension named above; an argument that names none is the same for every part. Nothing has to cross between parts.
Inputs may be any that keep to these rules, and one draw needn't show every extreme that they name: `rp_vectors`: distinct integer lattice vectors, no two columns equal. `re_vectors`: distinct integer lattice vectors, no two columns equal.
All inputs are finite; a program needn't handle non-finite values.
Results may differ from the reference program's by a relative error of at most 0.0038.
Values may be sent and summed in bfloat16 or wider, within the bound.
No kernel may reach another device: no remote copies, remote signals or barrier semaphores. Data moves between devices by JAX's collectives and lax.ppermute only.
A program may use at most 128 MiB of HBM per device.

```python
import math
import jax
import jax.numpy as jnp
from jax import lax

NW = 16
NM = 48
NFINE = 48
SPAN = 6
RP = 256
RE = 8
Q = 8
K = 2


def distinct_vectors(key, count):
    side = 2 * SPAN + 1
    total = side * side * side
    inner = jax.random.permutation(jax.random.fold_in(key, 11), total - 2).astype(jnp.int32) + 1
    corners = jnp.array([0, total - 1], dtype=jnp.int32)
    chosen = jnp.concatenate([corners, inner])[:count]
    order = jax.random.permutation(jax.random.fold_in(key, 13), count)
    chosen = chosen[order]
    first = chosen // (side * side)
    second = chosen // side % side
    third = chosen % side
    return (jnp.stack([first, second, third], axis=0) - SPAN).astype(jnp.int32)


def draw_rp_vectors(key, part):
    return distinct_vectors(jax.random.fold_in(key, 101), RP)


def draw_re_vectors(key, part):
    return distinct_vectors(jax.random.fold_in(key, 202), RE)


def with_ends(entries, key, least, high):
    index_at = [jax.random.randint(jax.random.fold_in(key, axis), (), 0, length) for axis, length in enumerate(entries.shape)]
    main_axis = entries.shape.index(max(entries.shape))
    neighbour = index_at[:main_axis] + [(index_at[main_axis] + 1) % entries.shape[main_axis]] + index_at[main_axis + 1:]
    return entries.at[tuple(index_at)].set(least).at[tuple(neighbour)].set(high)


def shard_levels(own_key, dims, cuts, low, largest):
    factor_of, own = 1.0, jax.random.fold_in(own_key, 6)
    for dim, blocks in cuts:
        steps = jnp.exp(jax.random.uniform(jax.random.fold_in(own, dim), (blocks,), jnp.float32, low / len(cuts), largest / len(cuts)))
        factor_of = factor_of * jnp.repeat(steps, dims[dim] // blocks).reshape([-1 if axis == dim else 1 for axis in range(len(dims))])
    return factor_of


def scatter_about(key, shape, spread, bound, split=(), kind=jnp.bfloat16):
    gain = shard_levels(key, shape, split, -0.22, 0.18) if split else 1.0
    result = jax.random.normal(key, shape, jnp.float32) * spread * gain
    return jnp.minimum(jnp.maximum(result, -bound), bound).astype(kind)


def setup_inputs(seed: int = 0, part: int = 0) -> dict:
    key_of = jax.random.split(jax.random.key(seed), 7)
    own_keys = jax.random.split(jax.random.fold_in(key_of[6], part), 7)
    return {
        "weights": scatter_about(key_of[0], (2, RP, RE, NM, NW * NW), (RP * RE) ** -0.5, 0.125, ((1, 8), (2, 2))),
        "rp_vectors": draw_rp_vectors(jax.random.fold_in(key_of[6], 71), part),
        "re_vectors": draw_re_vectors(jax.random.fold_in(key_of[6], 71), part),
        "q_points": with_ends(jax.random.randint(own_keys[3], (3, Q), 0, NFINE), jax.random.fold_in(own_keys[3], 1), 0, NFINE - 1).astype(jnp.int32),
        "k_points": with_ends(jax.random.randint(own_keys[4], (3, K), 0, NFINE), jax.random.fold_in(own_keys[4], 1), 0, NFINE - 1).astype(jnp.int32),
        "eigvecs": scatter_about(own_keys[5], (Q, 2, NM, NM), (2 * NM) ** -0.5, 0.625, ((0, 8),), jnp.float32),
    }


def phase_pair(points, vectors):
    products = jnp.sum(points[:, :, None] * vectors[:, None, :], axis=0)
    wrapped = jnp.mod(products, NFINE)
    angles = wrapped.astype(jnp.float32) * (2.0 * math.pi / NFINE)
    return jnp.cos(angles), jnp.sin(angles)


def rp_product(cosine_rows, sine_rows, flat_rows):
    cos_half = cosine_rows.astype(jnp.bfloat16)
    sin_half = sine_rows.astype(jnp.bfloat16)
    upper_rows = jnp.concatenate([cos_half, -sin_half], axis=1)
    lower_rows = jnp.concatenate([sin_half, cos_half], axis=1)
    stacked = jnp.stack([upper_rows, lower_rows], axis=1).reshape(-1, upper_rows.shape[1])
    return jnp.dot(stacked, flat_rows, preferred_element_type=jnp.float32)


def mix_modes(operand, rotation):
    return jnp.einsum("qenm,qnv->qevm", operand, rotation, precision=lax.Precision.HIGHEST)


def rotate(source, vectors):
    real_part = mix_modes(source[:, 0], vectors[:, 0]) - mix_modes(source[:, 1], vectors[:, 1])
    imag_part = mix_modes(source[:, 0], vectors[:, 1]) + mix_modes(source[:, 1], vectors[:, 0])
    return jnp.stack([real_part, imag_part], axis=1)


def contract(matrix, values):
    return jnp.einsum("ke,qenm->qknm", matrix, values, precision=lax.Precision.HIGHEST)


def k_sum(phase_cos, phase_sin, source):
    real_part = contract(phase_cos, source[:, 0]) - contract(phase_sin, source[:, 1])
    imag_part = contract(phase_sin, source[:, 0]) + contract(phase_cos, source[:, 1])
    return jnp.stack([real_part, imag_part], axis=1)


def reference(weights, rp_vectors, re_vectors, q_points, k_points, eigvecs):
    rp_cosine, rp_sine = phase_pair(q_points, rp_vectors)
    flat_rows = weights.reshape(2 * RP, RE * NM * NW * NW)
    summed = rp_product(rp_cosine, rp_sine, flat_rows).reshape(Q, 2, RE, NM, NW * NW)
    rotated = rotate(summed, eigvecs)
    re_cosine, re_sine = phase_pair(k_points, re_vectors)
    return k_sum(re_cosine, re_sine, rotated).astype(jnp.bfloat16)
```

```python
import math

import jax
import jax.numpy as jnp
from jax import lax
from jax.experimental import pallas as pl
from jax.experimental.pallas import tpu as pltpu
from jax.sharding import PartitionSpec as P

NFINE = 48
ROWS = 16


def bit_order(bits, core):
    order = list(range(bits))
    if bits > 1 and core == 1:
        order[0], order[1] = order[1], order[0]
    return order


def swap_slot(slot, bits):
    if bits < 2:
        return slot
    high, low = (slot >> (bits - 1)) & 1, (slot >> (bits - 2)) & 1
    rest = slot & ((1 << (bits - 2)) - 1)
    return (low << (bits - 1)) | (high << (bits - 2)) | rest


def wrapped_angle(products):
    turns = jnp.floor((products + 0.5) * (1.0 / NFINE))
    return (products - NFINE * turns) * (2.0 * math.pi / NFINE)


def phase_kernel(bits, rp_name, re_name, q_ref, k_ref, ev_ref, rpv_ref, w_ref, keep_ref, send_ref, slabs, lhs, prod, sems):
    parts, points, slab, modes, pairs = w_ref.shape
    slots = keep_ref.shape[0]
    per_core = keep_ref.shape[1]
    chunks = modes // ROWS

    def fetch(c, e):
        return pltpu.make_async_copy(
            w_ref.at[:, :, e, pl.ds(c * ROWS, ROWS), :], slabs.at[c, e], sems.at[c, e]
        )

    for c in range(chunks):
        for e in range(slab):
            fetch(c, e).start()

    me = lax.axis_index(rp_name)
    core = lax.axis_index(re_name)
    width = points * ROWS
    spread = (
        lax.broadcasted_iota(jnp.int32, (points, width), 1) // ROWS
        == lax.broadcasted_iota(jnp.int32, (points, width), 0)
    ).astype(jnp.bfloat16)
    vectors = jnp.dot(rpv_ref[...].astype(jnp.bfloat16), spread, preferred_element_type=jnp.float32)
    rows = []
    for slot in range(slots):
        offset = 0
        for at, (one, other) in enumerate(zip(bit_order(bits, 0), bit_order(bits, 1))):
            if (slot >> (bits - 1 - at)) & 1:
                offset = offset + jnp.where(core == 0, 1 << one, 1 << other)
        q = me ^ offset
        row = 0.0
        for axis in range(3):
            row = row + q_ref[axis, q].astype(jnp.float32) * vectors[axis : axis + 1, :]
        rows.append(row)
    angles = wrapped_angle(jnp.concatenate(rows, axis=0))
    cosine, sine = jnp.cos(angles), jnp.sin(angles)
    diagonal = (
        lax.broadcasted_iota(jnp.int32, (ROWS, width), 1) % ROWS
        == lax.broadcasted_iota(jnp.int32, (ROWS, width), 0)
    ).astype(jnp.float32)
    for slot in range(slots):
        cos_block = (cosine[slot : slot + 1] * diagonal).astype(jnp.bfloat16)
        sin_block = (sine[slot : slot + 1] * diagonal).astype(jnp.bfloat16)
        top, bottom = pl.ds(2 * slot * ROWS, ROWS), pl.ds((2 * slot + 1) * ROWS, ROWS)
        lhs[top, :width] = cos_block
        lhs[top, width:] = -sin_block
        lhs[bottom, :width] = sin_block
        lhs[bottom, width:] = cos_block

    places = (2 * per_core, slab)
    at_row = lax.broadcasted_iota(jnp.int32, places, 0)
    at_lane = lax.broadcasted_iota(jnp.int32, places, 1)
    products = jnp.zeros(places, jnp.float32)
    for side in range(2):
        for i in range(per_core):
            k = (core ^ side) * per_core + i
            for e in range(slab):
                total = 0
                for axis in range(3):
                    total = total + k_ref[axis, k] * ev_ref[axis, core * slab + e]
                here = (at_row == side * per_core + i) & (at_lane == e)
                products = jnp.where(here, total.astype(jnp.float32), products)
    k_angles = wrapped_angle(products)
    k_cos, k_sin = jnp.cos(k_angles), jnp.sin(k_angles)

    for c in range(chunks):
        for e in range(slab):
            fetch(c, e).wait()
            block = slabs[c, e].reshape(parts * width, pairs)
            prod[e] = jnp.dot(lhs[...], block, preferred_element_type=jnp.float32)
        for side in range(2):
            for i in range(per_core):
                line = side * per_core + i
                for slot in range(slots):
                    real = imag = None
                    for e in range(slab):
                        cos_e = jnp.broadcast_to(k_cos[line : line + 1, e : e + 1], (ROWS, pairs))
                        sin_e = jnp.broadcast_to(k_sin[line : line + 1, e : e + 1], (ROWS, pairs))
                        p_real = prod[e, pl.ds(2 * slot * ROWS, ROWS), :]
                        p_imag = prod[e, pl.ds((2 * slot + 1) * ROWS, ROWS), :]
                        r_term = cos_e * p_real - sin_e * p_imag
                        i_term = sin_e * p_real + cos_e * p_imag
                        real = r_term if real is None else real + r_term
                        imag = i_term if imag is None else imag + i_term
                    where = pl.ds(c * ROWS, ROWS)
                    if side == 0:
                        keep_ref[slot, i, 0, where, :] = real
                        keep_ref[slot, i, 1, where, :] = imag
                    else:
                        there = swap_slot(slot, bits)
                        send_ref[there, i, 0, where, :] = real.astype(send_ref.dtype)
                        send_ref[there, i, 1, where, :] = imag.astype(send_ref.dtype)


def rotate_kernel(mine_ref, got_ref, eig_ref, out_ref):
    real_vec, imag_vec = eig_ref[0, 0], eig_ref[0, 1]

    def mix(vec, source):
        return lax.dot_general(
            vec, source, (((0,), (0,)), ((), ())),
            precision=lax.Precision.HIGHEST, preferred_element_type=jnp.float32,
        )

    for i in range(mine_ref.shape[1]):
        real = mine_ref[0, i, 0] + got_ref[0, i, 0].astype(jnp.float32)
        imag = mine_ref[0, i, 1] + got_ref[0, i, 1].astype(jnp.float32)
        out_ref[0, 0, i] = (mix(real_vec, real) - mix(imag_vec, imag)).astype(out_ref.dtype)
        out_ref[0, 1, i] = (mix(imag_vec, real) + mix(real_vec, imag)).astype(out_ref.dtype)


def make_shards(mesh):
    ranks, cores = mesh.shape["rp"], mesh.shape["re"]
    bits = ranks.bit_length() - 1
    vmem = pl.BlockSpec(memory_space=pltpu.VMEM)
    smem = pl.BlockSpec(memory_space=pltpu.SMEM)

    def shards(weights, rp_vectors, re_vectors, q_points, k_points, eigvecs):
        parts, points, slab, modes, pairs = weights.shape
        slots = q_points.shape[1]
        per_core = k_points.shape[1] // cores
        chunks = modes // ROWS
        shape = (slots, per_core, 2, modes, pairs)
        keep, send = pl.pallas_call(
            lambda *refs: phase_kernel(bits, "rp", "re", *refs),
            out_shape=(jax.ShapeDtypeStruct(shape, jnp.float32), jax.ShapeDtypeStruct(shape, jnp.bfloat16)),
            in_specs=[smem, smem, smem, vmem, pl.BlockSpec(memory_space=pl.ANY)],
            out_specs=(vmem, vmem),
            scratch_shapes=[
                pltpu.VMEM((chunks, slab, parts, points, ROWS, pairs), jnp.bfloat16),
                pltpu.VMEM((2 * slots * ROWS, parts * points * ROWS), jnp.bfloat16),
                pltpu.VMEM((slab, 2 * slots * ROWS, pairs), jnp.float32),
                pltpu.SemaphoreType.DMA((chunks, slab)),
            ],
            compiler_params=pltpu.CompilerParams(vmem_limit_bytes=40 * 2**20),
            name="phase_sums",
        )(q_points, k_points, re_vectors, rp_vectors, weights)
        got = lax.ppermute(send, "re", [(c, c ^ 1) for c in range(cores)])
        mine = keep
        for step in range(bits):
            half = mine.shape[0] // 2
            total = mine + got.astype(jnp.float32)
            mine, away = total[:half], total[half:].astype(jnp.bfloat16)
            pairs_of = [
                (r * cores + c, (r ^ (1 << bit_order(bits, c)[step])) * cores + c)
                for r in range(ranks)
                for c in range(cores)
            ]
            got = lax.ppermute(away, ("rp", "re"), pairs_of)
        return pl.pallas_call(
            rotate_kernel,
            out_shape=jax.ShapeDtypeStruct((1, 2, per_core, modes, pairs), jnp.bfloat16),
            in_specs=[vmem, vmem, vmem],
            out_specs=vmem,
            name="rotate_modes",
        )(mine, got, eigvecs)

    return shards


def solution(mesh):
    return jax.shard_map(
        make_shards(mesh),
        mesh=mesh,
        in_specs=(
            P(None, "rp", "re", None, None),
            P(None, "rp"),
            P(),
            P(None, "grp"),
            P(None, "grp"),
            P(("grp", "rp"), None, None, None),
        ),
        out_specs=P(("grp", "rp"), None, "re", None, None),
        check_vma=False,
    )
```

```python
import math

import jax
import jax.numpy as jnp
from jax import lax
from jax.experimental import pallas as pl
from jax.experimental.pallas import tpu as pltpu
from jax.sharding import PartitionSpec as P

NFINE = 48
ROWS = 16


def bit_order(bits, core):
    order = list(range(bits))
    if bits > 1 and core == 1:
        order[0], order[1] = order[1], order[0]
    return order


def swap_slot(slot, bits):
    if bits < 2:
        return slot
    high, low = (slot >> (bits - 1)) & 1, (slot >> (bits - 2)) & 1
    rest = slot & ((1 << (bits - 2)) - 1)
    return (low << (bits - 1)) | (high << (bits - 2)) | rest


def wrapped_angle(products):
    turns = jnp.floor((products + 0.5) * (1.0 / NFINE))
    return (products - NFINE * turns) * (2.0 * math.pi / NFINE)


def phase_kernel(bits, q_hbm, k_hbm, ev_hbm, rpv_hbm, eig_hbm, w_ref, keep_ref, send_ref, mixer_ref,
                 slabs, lhs, prod, rpv_ref, eig_ref, q_ref, k_ref, ev_ref, sems, small_sems):
    parts, points, slab, modes, pairs = w_ref.shape
    slots, per_core = keep_ref.shape[:2]
    chunks = modes // ROWS

    small = [
        pltpu.make_async_copy(source, target, small_sems.at[at])
        for at, (source, target) in enumerate(
            [(rpv_hbm, rpv_ref), (q_hbm, q_ref), (k_hbm, k_ref), (ev_hbm, ev_ref), (eig_hbm, eig_ref)]
        )
    ]
    for copy in small:
        copy.start()

    def fetch(c, e):
        return pltpu.make_async_copy(
            w_ref.at[:, :, e, pl.ds(c * ROWS, ROWS), :], slabs.at[c, e], sems.at[c, e]
        )

    for c in range(chunks):
        for e in range(slab):
            fetch(c, e).start()
    for copy in small:
        copy.wait()

    me = lax.axis_index("rp")
    core = lax.axis_index("re")
    width = points * ROWS
    spread = (
        lax.broadcasted_iota(jnp.int32, (points, width), 1) // ROWS
        == lax.broadcasted_iota(jnp.int32, (points, width), 0)
    ).astype(jnp.bfloat16)
    vectors = jnp.dot(rpv_ref[...].astype(jnp.bfloat16), spread, preferred_element_type=jnp.float32)
    rows = []
    for slot in range(slots):
        offset = 0
        for at, (one, other) in enumerate(zip(bit_order(bits, 0), bit_order(bits, 1))):
            if (slot >> (bits - 1 - at)) & 1:
                offset = offset + jnp.where(core == 0, 1 << one, 1 << other)
        q = me ^ offset
        row = 0.0
        for axis in range(3):
            row = row + q_ref[axis, q].astype(jnp.float32) * vectors[axis : axis + 1, :]
        rows.append(row)
    angles = wrapped_angle(jnp.concatenate(rows, axis=0))
    cosine, sine = jnp.cos(angles), jnp.sin(angles)
    diagonal = (
        lax.broadcasted_iota(jnp.int32, (ROWS, width), 1) % ROWS
        == lax.broadcasted_iota(jnp.int32, (ROWS, width), 0)
    ).astype(jnp.float32)
    for slot in range(slots):
        cos_block = (cosine[slot : slot + 1] * diagonal).astype(jnp.bfloat16)
        sin_block = (sine[slot : slot + 1] * diagonal).astype(jnp.bfloat16)
        top, bottom = pl.ds(2 * slot * ROWS, ROWS), pl.ds((2 * slot + 1) * ROWS, ROWS)
        lhs[top, :width] = cos_block
        lhs[top, width:] = -sin_block
        lhs[bottom, :width] = sin_block
        lhs[bottom, width:] = cos_block

    places = (2 * per_core, slab)
    at_row = lax.broadcasted_iota(jnp.int32, places, 0)
    at_lane = lax.broadcasted_iota(jnp.int32, places, 1)
    products = jnp.zeros(places, jnp.float32)
    for side in range(2):
        for i in range(per_core):
            k = (core ^ side) * per_core + i
            for e in range(slab):
                total = 0
                for axis in range(3):
                    total = total + k_ref[k, axis] * ev_ref[axis, core * slab + e]
                here = (at_row == side * per_core + i) & (at_lane == e)
                products = jnp.where(here, total.astype(jnp.float32), products)
    k_angles = wrapped_angle(products)
    k_cos, k_sin = jnp.cos(k_angles), jnp.sin(k_angles)

    real_vec, imag_vec = eig_ref[0, 0], eig_ref[0, 1]
    rotation = jnp.concatenate(
        [jnp.concatenate([real_vec, imag_vec], axis=1), jnp.concatenate([-imag_vec, real_vec], axis=1)], axis=0
    )
    high = rotation.astype(jnp.bfloat16)
    mixer_ref[0] = high
    mixer_ref[1] = high
    mixer_ref[2] = (rotation - high.astype(jnp.float32)).astype(jnp.bfloat16)

    def k_sum(c):
        where = pl.ds(c * ROWS, ROWS)
        for slot in range(slots):
            sums = {}
            for e in range(slab):
                p_real = prod[c % 2, e, pl.ds(2 * slot * ROWS, ROWS), :]
                p_imag = prod[c % 2, e, pl.ds((2 * slot + 1) * ROWS, ROWS), :]
                for line in range(2 * per_core):
                    cos_e = jnp.broadcast_to(k_cos[line : line + 1, e : e + 1], (ROWS, pairs))
                    sin_e = jnp.broadcast_to(k_sin[line : line + 1, e : e + 1], (ROWS, pairs))
                    r_term = cos_e * p_real - sin_e * p_imag
                    i_term = sin_e * p_real + cos_e * p_imag
                    if e:
                        r_term, i_term = r_term + sums[line][0], i_term + sums[line][1]
                    sums[line] = r_term, i_term
            for i in range(per_core):
                for part in range(2):
                    keep_ref[slot, i, part, where, :] = sums[i][part]
                    send_ref[swap_slot(slot, bits), i, part, where, :] = sums[per_core + i][part].astype(send_ref.dtype)

    for c in range(chunks):
        for e in range(slab):
            fetch(c, e).wait()
        for e in range(slab):
            prod[c % 2, e] = jnp.dot(
                lhs[...], slabs[c, e].reshape(parts * width, pairs), preferred_element_type=jnp.float32
            )
        if c:
            k_sum(c - 1)
    k_sum(chunks - 1)


def rotate_kernel(mine_ref, got_ref, mixer_ref, out_ref):
    modes, pairs = mine_ref.shape[-2:]
    mixer = mixer_ref[...].reshape(-1, 2 * modes)
    for i in range(mine_ref.shape[1]):
        source = (mine_ref[0, i] + got_ref[0, i].astype(jnp.float32)).reshape(2 * modes, pairs)
        high = source.astype(jnp.bfloat16)
        low = (source - high.astype(jnp.float32)).astype(jnp.bfloat16)
        stacked = jnp.concatenate([high, low, high], axis=0)
        turned = lax.dot_general(
            mixer, stacked, (((0,), (0,)), ((), ())), preferred_element_type=jnp.float32
        ).astype(out_ref.dtype)
        out_ref[0, 0, i] = turned[:modes]
        out_ref[0, 1, i] = turned[modes:]


def make_shards(mesh):
    ranks, cores = mesh.shape["rp"], mesh.shape["re"]
    bits = ranks.bit_length() - 1
    vmem = pl.BlockSpec(memory_space=pltpu.VMEM)
    smem = pl.BlockSpec(memory_space=pltpu.SMEM)

    def shards(weights, rp_vectors, re_vectors, q_points, k_points, eigvecs):
        parts, points, slab, modes, pairs = weights.shape
        slots = q_points.shape[1]
        per_core = k_points.shape[1] // cores
        chunks = modes // ROWS
        shape = (slots, per_core, 2, modes, pairs)
        hbm = pl.BlockSpec(memory_space=pltpu.HBM)
        keep, send, mixer = pl.pallas_call(
            lambda *refs: phase_kernel(bits, *refs),
            out_shape=(
                jax.ShapeDtypeStruct(shape, jnp.float32),
                jax.ShapeDtypeStruct(shape, jnp.bfloat16),
                jax.ShapeDtypeStruct((3, 2 * modes, 2 * modes), jnp.bfloat16),
            ),
            in_specs=[hbm] * 6,
            out_specs=(vmem, vmem, vmem),
            scratch_shapes=[
                pltpu.VMEM((chunks, slab, parts, points, ROWS, pairs), jnp.bfloat16),
                pltpu.VMEM((2 * slots * ROWS, parts * points * ROWS), jnp.bfloat16),
                pltpu.VMEM((2, slab, 2 * slots * ROWS, pairs), jnp.float32),
                pltpu.VMEM(rp_vectors.shape, jnp.int32),
                pltpu.VMEM(eigvecs.shape, jnp.float32),
                pltpu.SMEM(q_points.shape, jnp.int32),
                pltpu.SMEM(k_points.shape[::-1], jnp.int32),
                pltpu.SMEM(re_vectors.shape, jnp.int32),
                pltpu.SemaphoreType.DMA((chunks, slab)),
                pltpu.SemaphoreType.DMA((5,)),
            ],
            compiler_params=pltpu.CompilerParams(vmem_limit_bytes=32 * 2**20),
            name="phase_sums",
        )(*[pltpu.with_memory_space_constraint(x, pltpu.HBM) for x in (q_points, k_points.T, re_vectors, rp_vectors, eigvecs, weights)])
        got = lax.ppermute(send, "re", [(c, c ^ 1) for c in range(cores)])
        mine = keep
        for step in range(bits):
            half = slots >> (step + 1)
            mine = mine[: 2 * half] + got.astype(jnp.float32)
            away = mine[half:].astype(jnp.bfloat16)
            pairs_of = [
                (r * cores + c, (r ^ (1 << bit_order(bits, c)[step])) * cores + c)
                for r in range(ranks)
                for c in range(cores)
            ]
            got = lax.ppermute(away, ("rp", "re"), pairs_of)
        return pl.pallas_call(
            rotate_kernel,
            out_shape=jax.ShapeDtypeStruct((1, 2, per_core, modes, pairs), jnp.bfloat16),
            in_specs=[vmem, vmem, vmem],
            out_specs=vmem,
            compiler_params=pltpu.CompilerParams(vmem_limit_bytes=4 * 2**20),
            name="rotate_modes",
        )(mine, got, mixer)

    return shards


def solution(mesh):
    return jax.shard_map(
        make_shards(mesh),
        mesh=mesh,
        in_specs=(
            P(None, "rp", "re", None, None),
            P(None, "rp"),
            P(),
            P(None, "grp"),
            P(None, "grp"),
            P(("grp", "rp"), None, None, None),
        ),
        out_specs=P(("grp", "rp"), None, "re", None, None),
        check_vma=False,
    )
```

```python
import math

import jax
import jax.numpy as jnp
from jax import lax
from jax.experimental import pallas as pl
from jax.experimental.pallas import tpu as pltpu
from jax.sharding import PartitionSpec as P

NFINE = 48
NEAR = 2
PIECES = 2
ROWS = 16


def slot_offset(slot, bits):
    near = min(NEAR, bits - 1)
    return (slot >> (bits - near)) | ((slot & ((1 << (bits - near)) - 1)) << near)


def wrapped_angle(products):
    turns = jnp.floor((products + 0.5) * (1.0 / NFINE))
    return (products - NFINE * turns) * (2.0 * math.pi / NFINE)


def k_phases(core, per_core, slab, k_ref, ev_ref):
    places = (2 * per_core, slab)
    at_row = lax.broadcasted_iota(jnp.int32, places, 0)
    at_lane = lax.broadcasted_iota(jnp.int32, places, 1)
    products = jnp.zeros(places, jnp.float32)
    for line in range(2 * per_core):
        k = (core ^ (line // per_core)) * per_core + line % per_core
        for e in range(slab):
            total = 0
            for axis in range(3):
                total = total + k_ref[k, axis] * ev_ref[axis, core * slab + e]
            products = jnp.where((at_row == line) & (at_lane == e), total.astype(jnp.float32), products)
    angles = wrapped_angle(products)
    return jnp.cos(angles), jnp.sin(angles)


def k_sum(prod_ref, c, slot, k_cos, k_sin, line):
    slab, _, pairs = prod_ref.shape[1:]
    real = imag = None
    for e in range(slab):
        p_real = prod_ref[c, e, pl.ds(2 * slot * ROWS, ROWS), :]
        p_imag = prod_ref[c, e, pl.ds((2 * slot + 1) * ROWS, ROWS), :]
        cos_e = jnp.broadcast_to(k_cos[line : line + 1, e : e + 1], (ROWS, pairs))
        sin_e = jnp.broadcast_to(k_sin[line : line + 1, e : e + 1], (ROWS, pairs))
        r_term = cos_e * p_real - sin_e * p_imag
        i_term = sin_e * p_real + cos_e * p_imag
        real = r_term if e == 0 else real + r_term
        imag = i_term if e == 0 else imag + i_term
    return real, imag


def phase_kernel(bits, q_hbm, k_hbm, ev_hbm, rpv_hbm, w_ref, prod_ref, send_ref, turn_ref,
                 slabs, lhs, rpv_ref, q_ref, k_ref, ev_ref, sems, small_sems):
    parts, points, slab, modes, pairs = w_ref.shape
    slots, per_core = send_ref.shape[:2]
    chunks = modes // ROWS
    pieces = sems.shape[1]

    small = [
        pltpu.make_async_copy(source, target, small_sems.at[at])
        for at, (source, target) in enumerate(
            [(rpv_hbm, rpv_ref), (q_hbm, q_ref), (k_hbm, k_ref), (ev_hbm, ev_ref)]
        )
    ]
    for copy in small:
        copy.start()

    def fetch(c, piece):
        some = pl.ds(piece * (points // pieces), points // pieces)
        return pltpu.make_async_copy(
            w_ref.at[:, some, :, pl.ds(c * ROWS, ROWS), :], slabs.at[c, :, some], sems.at[c, piece]
        )

    for c in range(chunks):
        for piece in range(pieces):
            fetch(c, piece).start()
    for copy in small:
        copy.wait()

    me = lax.axis_index("rp")
    core = lax.axis_index("re")
    width = points * ROWS
    spread = (
        lax.broadcasted_iota(jnp.int32, (points, width), 1) // ROWS
        == lax.broadcasted_iota(jnp.int32, (points, width), 0)
    ).astype(jnp.bfloat16)
    vectors = jnp.dot(rpv_ref[...].astype(jnp.bfloat16), spread, preferred_element_type=jnp.float32)
    rows = []
    for slot in range(slots):
        q = me ^ slot_offset(slot, bits)
        row = 0.0
        for axis in range(3):
            row = row + q_ref[axis, q].astype(jnp.float32) * vectors[axis : axis + 1, :]
        rows.append(row)
    angles = wrapped_angle(jnp.concatenate(rows, axis=0))
    cosine, sine = jnp.cos(angles), jnp.sin(angles)
    diagonal = (
        lax.broadcasted_iota(jnp.int32, (ROWS, width), 1) % ROWS
        == lax.broadcasted_iota(jnp.int32, (ROWS, width), 0)
    ).astype(jnp.float32)
    for slot in range(slots):
        cos_block = (cosine[slot : slot + 1] * diagonal).astype(jnp.bfloat16)
        sin_block = (sine[slot : slot + 1] * diagonal).astype(jnp.bfloat16)
        top, bottom = pl.ds(2 * slot * ROWS, ROWS), pl.ds((2 * slot + 1) * ROWS, ROWS)
        lhs[top, :width] = cos_block
        lhs[top, width:] = -sin_block
        lhs[bottom, :width] = sin_block
        lhs[bottom, width:] = cos_block

    k_cos, k_sin = k_phases(core, per_core, slab, k_ref, ev_ref)
    turn_ref[0] = k_cos
    turn_ref[1] = k_sin

    def send_sum(c):
        for slot in range(slots):
            for i in range(per_core):
                sums = k_sum(prod_ref, c, slot, k_cos, k_sin, per_core + i)
                for part in range(2):
                    send_ref[slot, i, part, pl.ds(c * ROWS, ROWS), :] = sums[part].astype(send_ref.dtype)

    for c in range(chunks):
        for piece in range(pieces):
            fetch(c, piece).wait()
        for e in range(slab):
            block = slabs[c, :, :, e].reshape(parts * width, pairs)
            prod_ref[c, e] = jnp.dot(lhs[...], block, preferred_element_type=jnp.float32)
        if c:
            send_sum(c - 1)
    send_sum(chunks - 1)


def keep_kernel(prod_ref, turn_ref, eig_hbm, keep_ref, mixer_ref, eig_ref, sem):
    fetch = pltpu.make_async_copy(eig_hbm, eig_ref, sem)
    fetch.start()
    slots, per_core = keep_ref.shape[:2]
    k_cos, k_sin = turn_ref[0], turn_ref[1]
    for c in range(prod_ref.shape[0]):
        for slot in range(slots):
            for i in range(per_core):
                sums = k_sum(prod_ref, c, slot, k_cos, k_sin, i)
                for part in range(2):
                    keep_ref[slot, i, part, pl.ds(c * ROWS, ROWS), :] = sums[part]

    fetch.wait()
    real_vec, imag_vec = eig_ref[0, 0], eig_ref[0, 1]
    rotation = jnp.concatenate(
        [jnp.concatenate([real_vec, imag_vec], axis=1), jnp.concatenate([-imag_vec, real_vec], axis=1)], axis=0
    )
    high = rotation.astype(jnp.bfloat16)
    mixer_ref[0] = high
    mixer_ref[1] = high
    mixer_ref[2] = (rotation - high.astype(jnp.float32)).astype(jnp.bfloat16)


def rotate_kernel(mine_ref, got_ref, mixer_ref, out_ref):
    modes, pairs = mine_ref.shape[-2:]
    mixer = mixer_ref[...].reshape(-1, 2 * modes)
    for i in range(mine_ref.shape[1]):
        source = (mine_ref[0, i] + got_ref[0, i].astype(jnp.float32)).reshape(2 * modes, pairs)
        high = source.astype(jnp.bfloat16)
        low = (source - high.astype(jnp.float32)).astype(jnp.bfloat16)
        stacked = jnp.concatenate([high, low, high], axis=0)
        turned = lax.dot_general(
            mixer, stacked, (((0,), (0,)), ((), ())), preferred_element_type=jnp.float32
        ).astype(out_ref.dtype)
        out_ref[0, 0, i] = turned[:modes]
        out_ref[0, 1, i] = turned[modes:]


def make_shards(mesh):
    ranks, cores = mesh.shape["rp"], mesh.shape["re"]
    bits = ranks.bit_length() - 1
    vmem = pl.BlockSpec(memory_space=pltpu.VMEM)
    hbm = pl.BlockSpec(memory_space=pltpu.HBM)

    def in_hbm(x):
        return pltpu.with_memory_space_constraint(x, pltpu.HBM)

    def shards(weights, rp_vectors, re_vectors, q_points, k_points, eigvecs):
        parts, points, slab, modes, pairs = weights.shape
        slots = q_points.shape[1]
        per_core = k_points.shape[1] // cores
        chunks = modes // ROWS
        shape = (slots, per_core, 2, modes, pairs)
        pieces = math.gcd(points, PIECES)
        lines = 2 * slots * ROWS
        prod, send, turn = pl.pallas_call(
            lambda *refs: phase_kernel(bits, *refs),
            out_shape=(
                jax.ShapeDtypeStruct((chunks, slab, lines, pairs), jnp.float32),
                jax.ShapeDtypeStruct(shape, jnp.bfloat16),
                jax.ShapeDtypeStruct((2, 2 * per_core, slab), jnp.float32),
            ),
            in_specs=[hbm] * 5,
            out_specs=(vmem, vmem, vmem),
            scratch_shapes=[
                pltpu.VMEM((chunks, parts, points, slab, ROWS, pairs), jnp.bfloat16),
                pltpu.VMEM((lines, parts * points * ROWS), jnp.bfloat16),
                pltpu.VMEM(rp_vectors.shape, jnp.int32),
                pltpu.SMEM(q_points.shape, jnp.int32),
                pltpu.SMEM(k_points.shape[::-1], jnp.int32),
                pltpu.SMEM(re_vectors.shape, jnp.int32),
                pltpu.SemaphoreType.DMA((chunks, pieces)),
                pltpu.SemaphoreType.DMA((4,)),
            ],
            compiler_params=pltpu.CompilerParams(vmem_limit_bytes=32 * 2**20),
            name="phase_sums",
        )(*[in_hbm(x) for x in (q_points, k_points.T, re_vectors, rp_vectors, weights)])
        keep, mixer = pl.pallas_call(
            keep_kernel,
            out_shape=(
                jax.ShapeDtypeStruct(shape, jnp.float32),
                jax.ShapeDtypeStruct((3, 2 * modes, 2 * modes), jnp.bfloat16),
            ),
            in_specs=[vmem, vmem, hbm],
            out_specs=(vmem, vmem),
            scratch_shapes=[pltpu.VMEM(eigvecs.shape, jnp.float32), pltpu.SemaphoreType.DMA],
            compiler_params=pltpu.CompilerParams(vmem_limit_bytes=4 * 2**20),
            cost_estimate=pl.CostEstimate(flops=8 * prod.size, bytes_accessed=4 * prod.size, transcendentals=0),
            name="own_k_sums",
        )(prod, turn, in_hbm(eigvecs))
        got = lax.ppermute(send, "re", [(c, c ^ 1) for c in range(cores)])
        mine = keep + got.astype(jnp.float32)

        def swap(block, offset):
            return lax.ppermute(block, "rp", [(r, r ^ offset) for r in range(ranks)]).astype(jnp.float32)

        near = min(NEAR, bits - 1)
        far = bits - near
        half = slots >> near
        parcels = {d: mine[d * half : (d + 1) * half].astype(jnp.bfloat16) for d in range(1, 1 << near)}
        total = mine[:half]
        for d in sorted(parcels, key=lambda d: -d):
            total = total + swap(parcels[d], d)
        for step in range(far - 1):
            half = half // 2
            total = total[:half] + swap(total[half : 2 * half].astype(jnp.bfloat16), 1 << (bits - 1 - step))
        got = lax.ppermute(total[half // 2 :].astype(jnp.bfloat16), "rp", [(r, r ^ (1 << near)) for r in range(ranks)])
        return pl.pallas_call(
            rotate_kernel,
            out_shape=jax.ShapeDtypeStruct((1, 2, per_core, modes, pairs), jnp.bfloat16),
            in_specs=[vmem, vmem, vmem],
            out_specs=vmem,
            compiler_params=pltpu.CompilerParams(vmem_limit_bytes=4 * 2**20),
            name="rotate_modes",
        )(total, got, mixer)

    return shards


def solution(mesh):
    return jax.shard_map(
        make_shards(mesh),
        mesh=mesh,
        in_specs=(
            P(None, "rp", "re", None, None),
            P(None, "rp"),
            P(),
            P(None, "grp"),
            P(None, "grp"),
            P(("grp", "rp"), None, None, None),
        ),
        out_specs=P(("grp", "rp"), None, "re", None, None),
        check_vma=False,
    )
```

```python
import math

import jax
import jax.numpy as jnp
from jax import lax
from jax.experimental import pallas as pl
from jax.experimental.pallas import tpu as pltpu
from jax.sharding import PartitionSpec as P

NFINE = 48
NEAR = 2
PIECES = 2
ROWS = 16


def near_bits(bits):
    return min(NEAR, bits - 1)


def slot_offsets(bits):
    near = near_bits(bits)
    last = (1 << near) - 1
    beyond = [f << near for f in range(1, 1 << (bits - near))]
    return [last | far for far in (*beyond, 0)], [d | far for d in range(last) for far in beyond] + list(range(last))


def wrapped_angle(products):
    turns = jnp.floor((products + 0.5) * (1.0 / NFINE))
    return (products - NFINE * turns) * (2.0 * math.pi / NFINE)


def k_phases(core, per_core, slab, k_ref, ev_ref):
    places = (2 * per_core, slab)
    at_row = lax.broadcasted_iota(jnp.int32, places, 0)
    at_lane = lax.broadcasted_iota(jnp.int32, places, 1)
    products = jnp.zeros(places, jnp.float32)
    for line in range(2 * per_core):
        k = (core ^ (line // per_core)) * per_core + line % per_core
        for e in range(slab):
            total = 0
            for axis in range(3):
                total = total + k_ref[k, axis] * ev_ref[axis, core * slab + e]
            products = jnp.where((at_row == line) & (at_lane == e), total.astype(jnp.float32), products)
    angles = wrapped_angle(products)
    return jnp.cos(angles), jnp.sin(angles)


def k_sum(prod_ref, c, slot, k_cos, k_sin, line):
    slab, _, pairs = prod_ref.shape[1:]
    real = imag = None
    for e in range(slab):
        p_real = prod_ref[c, e, pl.ds(2 * slot * ROWS, ROWS), :]
        p_imag = prod_ref[c, e, pl.ds((2 * slot + 1) * ROWS, ROWS), :]
        cos_e = jnp.broadcast_to(k_cos[line : line + 1, e : e + 1], (ROWS, pairs))
        sin_e = jnp.broadcast_to(k_sin[line : line + 1, e : e + 1], (ROWS, pairs))
        r_term = cos_e * p_real - sin_e * p_imag
        i_term = sin_e * p_real + cos_e * p_imag
        real = r_term if e == 0 else real + r_term
        imag = i_term if e == 0 else imag + i_term
    return real, imag


def phase_kernel(bits, q_hbm, k_hbm, ev_hbm, rpv_hbm, w_ref, prod_ref, first_ref, rest_ref, turn_ref,
                 slabs, lhs, rpv_ref, q_ref, k_ref, ev_ref, sems, small_sems):
    parts, points, slab, modes, pairs = w_ref.shape
    first_slots, per_core = first_ref.shape[:2]
    slots = first_slots + rest_ref.shape[0]
    chunks = modes // ROWS
    pieces = sems.shape[1]

    small = [
        pltpu.make_async_copy(source, target, small_sems.at[at])
        for at, (source, target) in enumerate(
            [(rpv_hbm, rpv_ref), (q_hbm, q_ref), (k_hbm, k_ref), (ev_hbm, ev_ref)]
        )
    ]
    for copy in small:
        copy.start()

    def fetch(c, piece):
        some = pl.ds(piece * (points // pieces), points // pieces)
        return pltpu.make_async_copy(
            w_ref.at[:, some, :, pl.ds(c * ROWS, ROWS), :], slabs.at[c, :, some], sems.at[c, piece]
        )

    for c in range(chunks):
        for piece in range(pieces):
            fetch(c, piece).start()
    for copy in small:
        copy.wait()

    me = lax.axis_index("rp")
    core = lax.axis_index("re")
    width = points * ROWS
    spread = (
        lax.broadcasted_iota(jnp.int32, (points, width), 1) // ROWS
        == lax.broadcasted_iota(jnp.int32, (points, width), 0)
    ).astype(jnp.bfloat16)
    vectors = jnp.dot(rpv_ref[...].astype(jnp.bfloat16), spread, preferred_element_type=jnp.float32)
    rows = []
    for offset in sum(slot_offsets(bits), []):
        q = me ^ offset
        row = 0.0
        for axis in range(3):
            row = row + q_ref[axis, q].astype(jnp.float32) * vectors[axis : axis + 1, :]
        rows.append(row)
    angles = wrapped_angle(jnp.concatenate(rows, axis=0))
    cosine, sine = jnp.cos(angles), jnp.sin(angles)
    diagonal = (
        lax.broadcasted_iota(jnp.int32, (ROWS, width), 1) % ROWS
        == lax.broadcasted_iota(jnp.int32, (ROWS, width), 0)
    ).astype(jnp.float32)
    for slot in range(slots):
        cos_block = (cosine[slot : slot + 1] * diagonal).astype(jnp.bfloat16)
        sin_block = (sine[slot : slot + 1] * diagonal).astype(jnp.bfloat16)
        top, bottom = pl.ds(2 * slot * ROWS, ROWS), pl.ds((2 * slot + 1) * ROWS, ROWS)
        lhs[top, :width] = cos_block
        lhs[top, width:] = -sin_block
        lhs[bottom, :width] = sin_block
        lhs[bottom, width:] = cos_block

    k_cos, k_sin = k_phases(core, per_core, slab, k_ref, ev_ref)
    turn_ref[0] = k_cos
    turn_ref[1] = k_sin

    def send_sum(c):
        for slot in range(slots):
            for i in range(per_core):
                sums = k_sum(prod_ref, c, slot, k_cos, k_sin, per_core + i)
                for part in range(2):
                    place = (i, part, pl.ds(c * ROWS, ROWS), slice(None))
                    if slot < first_slots:
                        first_ref[(slot, *place)] = sums[part].astype(first_ref.dtype)
                    else:
                        rest_ref[(slot - first_slots, *place)] = sums[part].astype(rest_ref.dtype)

    for c in range(chunks):
        for piece in range(pieces):
            fetch(c, piece).wait()
        for e in range(slab):
            block = slabs[c, :, :, e].reshape(parts * width, pairs)
            prod_ref[c, e] = jnp.dot(lhs[...], block, preferred_element_type=jnp.float32)
        if c:
            send_sum(c - 1)
    send_sum(chunks - 1)


def keep_kernel(prod_ref, turn_ref, eig_hbm, first_ref, rest_ref, mixer_ref, eig_ref, sem):
    fetch = pltpu.make_async_copy(eig_hbm, eig_ref, sem)
    fetch.start()
    first_slots, per_core = first_ref.shape[:2]
    slots = first_slots + rest_ref.shape[0]
    k_cos, k_sin = turn_ref[0], turn_ref[1]
    for c in range(prod_ref.shape[0]):
        for slot in range(slots):
            for i in range(per_core):
                sums = k_sum(prod_ref, c, slot, k_cos, k_sin, i)
                for part in range(2):
                    place = (i, part, pl.ds(c * ROWS, ROWS), slice(None))
                    if slot < first_slots:
                        first_ref[(slot, *place)] = sums[part]
                    else:
                        rest_ref[(slot - first_slots, *place)] = sums[part]

    fetch.wait()
    real_vec, imag_vec = eig_ref[0, 0], eig_ref[0, 1]
    rotation = jnp.concatenate(
        [jnp.concatenate([real_vec, imag_vec], axis=1), jnp.concatenate([-imag_vec, real_vec], axis=1)], axis=0
    )
    high = rotation.astype(jnp.bfloat16)
    mixer_ref[0] = high
    mixer_ref[1] = high
    mixer_ref[2] = (rotation - high.astype(jnp.float32)).astype(jnp.bfloat16)


def rotate_kernel(mixer_ref, mine_ref, *refs):
    *got_refs, out_ref = refs
    modes, pairs = mine_ref.shape[-2:]
    mixer = mixer_ref[...].reshape(-1, 2 * modes)
    for i in range(mine_ref.shape[1]):
        source = mine_ref[0, i]
        for got_ref in got_refs:
            source = source + got_ref[0, i].astype(jnp.float32)
        source = source.reshape(2 * modes, pairs)
        high = source.astype(jnp.bfloat16)
        low = (source - high.astype(jnp.float32)).astype(jnp.bfloat16)
        stacked = jnp.concatenate([high, low, high], axis=0)
        turned = lax.dot_general(
            mixer, stacked, (((0,), (0,)), ((), ())), preferred_element_type=jnp.float32
        ).astype(out_ref.dtype)
        out_ref[0, 0, i] = turned[:modes]
        out_ref[0, 1, i] = turned[modes:]


def make_shards(mesh):
    ranks, cores = mesh.shape["rp"], mesh.shape["re"]
    bits = ranks.bit_length() - 1
    vmem = pl.BlockSpec(memory_space=pltpu.VMEM)
    hbm = pl.BlockSpec(memory_space=pltpu.HBM)

    def in_hbm(x):
        return pltpu.with_memory_space_constraint(x, pltpu.HBM)

    def shards(weights, rp_vectors, re_vectors, q_points, k_points, eigvecs):
        parts, points, slab, modes, pairs = weights.shape
        slots = q_points.shape[1]
        per_core = k_points.shape[1] // cores
        chunks = modes // ROWS
        near = near_bits(bits)
        groups, spans = 1 << near, 1 << (bits - near)
        block = (per_core, 2, modes, pairs)
        shapes = [(spans, *block), (slots - spans, *block)]
        pieces = math.gcd(points, PIECES)
        lines = 2 * slots * ROWS
        prod, first_away, rest_away, turn = pl.pallas_call(
            lambda *refs: phase_kernel(bits, *refs),
            out_shape=(
                jax.ShapeDtypeStruct((chunks, slab, lines, pairs), jnp.float32),
                *[jax.ShapeDtypeStruct(shape, jnp.bfloat16) for shape in shapes],
                jax.ShapeDtypeStruct((2, 2 * per_core, slab), jnp.float32),
            ),
            in_specs=[hbm] * 5,
            out_specs=(vmem,) * 4,
            scratch_shapes=[
                pltpu.VMEM((chunks, parts, points, slab, ROWS, pairs), jnp.bfloat16),
                pltpu.VMEM((lines, parts * points * ROWS), jnp.bfloat16),
                pltpu.VMEM(rp_vectors.shape, jnp.int32),
                pltpu.SMEM(q_points.shape, jnp.int32),
                pltpu.SMEM(k_points.shape[::-1], jnp.int32),
                pltpu.SMEM(re_vectors.shape, jnp.int32),
                pltpu.SemaphoreType.DMA((chunks, pieces)),
                pltpu.SemaphoreType.DMA((4,)),
            ],
            compiler_params=pltpu.CompilerParams(vmem_limit_bytes=32 * 2**20),
            name="phase_sums",
        )(*[in_hbm(x) for x in (q_points, k_points.T, re_vectors, rp_vectors, weights)])
        first_sums, rest_sums, mixer = pl.pallas_call(
            keep_kernel,
            out_shape=(
                *[jax.ShapeDtypeStruct(shape, jnp.float32) for shape in shapes],
                jax.ShapeDtypeStruct((3, 2 * modes, 2 * modes), jnp.bfloat16),
            ),
            in_specs=[vmem, vmem, hbm],
            out_specs=(vmem,) * 3,
            scratch_shapes=[pltpu.VMEM(eigvecs.shape, jnp.float32), pltpu.SemaphoreType.DMA],
            compiler_params=pltpu.CompilerParams(vmem_limit_bytes=4 * 2**20),
            cost_estimate=pl.CostEstimate(flops=8 * prod.size, bytes_accessed=4 * prod.size, transcendentals=0),
            name="own_k_sums",
        )(prod, turn, in_hbm(eigvecs))

        def swap(blocks, offset, axis="rp"):
            size = mesh.shape[axis]
            ends = [(r, r ^ offset) for r in range(size)]
            return lax.ppermute(blocks.astype(jnp.bfloat16), axis, ends)

        def wide(blocks):
            return blocks.astype(jnp.float32)

        first_other = swap(first_away, 1, "re")
        rest_other = swap(rest_away, 1, "re")
        last = groups - 1
        first_sums = first_sums + wide(first_other)
        rest_sums = rest_sums + wide(rest_other)
        first_got = swap(first_sums, last)
        width = spans - 1
        beyond = [swap(rest_sums[d * width : (d + 1) * width], d) for d in range(1, last)]
        among = [swap(rest_sums[last * width + d :][:1], d) for d in range(1, last)]
        total = rest_sums[:width] + wide(first_got[:width])
        for got in beyond:
            total = total + wide(got)
        own = rest_sums[last * width :][:1] + wide(first_got[width:])
        half = spans // 2
        while half > 1:
            got = swap(total[half - 1 :], half << near)
            total = total[: half - 1] + wide(got[1:])
            among.append(got[:1])
            half = half // 2
        among.append(swap(total, 1 << near))
        return pl.pallas_call(
            rotate_kernel,
            out_shape=jax.ShapeDtypeStruct((1, 2, per_core, modes, pairs), jnp.bfloat16),
            in_specs=[vmem] * (2 + len(among)),
            out_specs=vmem,
            compiler_params=pltpu.CompilerParams(vmem_limit_bytes=4 * 2**20),
            name="rotate_modes",
        )(mixer, own, *among)

    return shards


def solution(mesh):
    return jax.shard_map(
        make_shards(mesh),
        mesh=mesh,
        in_specs=(
            P(None, "rp", "re", None, None),
            P(None, "rp"),
            P(),
            P(None, "grp"),
            P(None, "grp"),
            P(("grp", "rp"), None, None, None),
        ),
        out_specs=P(("grp", "rp"), None, "re", None, None),
        check_vma=False,
    )
```

```python
import math

import jax
import jax.numpy as jnp
from jax import lax
from jax.experimental import pallas as pl
from jax.experimental.pallas import tpu as pltpu
from jax.sharding import PartitionSpec as P

NFINE = 48
NEAR = 2
PIECES = 2
ROWS = 16


def near_bits(bits):
    return min(NEAR, bits - 1)


def slot_offsets(bits):
    near = near_bits(bits)
    last = (1 << near) - 1
    beyond = [f << near for f in range(1, 1 << (bits - near))]
    return [last | far for far in (*beyond, 0)], [d | far for d in range(last) for far in beyond] + list(range(last))


def wrapped_angle(products):
    turns = jnp.floor((products + 0.5) * (1.0 / NFINE))
    return (products - NFINE * turns) * (2.0 * math.pi / NFINE)


def k_phases(core, per_core, slab, k_ref, ev_ref):
    places = (2 * per_core, slab)
    at_row = lax.broadcasted_iota(jnp.int32, places, 0)
    at_lane = lax.broadcasted_iota(jnp.int32, places, 1)
    products = jnp.zeros(places, jnp.float32)
    for line in range(2 * per_core):
        k = (core ^ (line // per_core)) * per_core + line % per_core
        for e in range(slab):
            total = 0
            for axis in range(3):
                total = total + k_ref[k, axis] * ev_ref[axis, core * slab + e]
            products = jnp.where((at_row == line) & (at_lane == e), total.astype(jnp.float32), products)
    angles = wrapped_angle(products)
    return jnp.cos(angles), jnp.sin(angles)


def k_sum(prod_ref, c, slot, k_cos, k_sin, line):
    slab, _, pairs = prod_ref.shape[1:]
    real = imag = None
    for e in range(slab):
        p_real = prod_ref[c, e, pl.ds(2 * slot * ROWS, ROWS), :]
        p_imag = prod_ref[c, e, pl.ds((2 * slot + 1) * ROWS, ROWS), :]
        cos_e = jnp.broadcast_to(k_cos[line : line + 1, e : e + 1], (ROWS, pairs))
        sin_e = jnp.broadcast_to(k_sin[line : line + 1, e : e + 1], (ROWS, pairs))
        r_term = cos_e * p_real - sin_e * p_imag
        i_term = sin_e * p_real + cos_e * p_imag
        real = r_term if e == 0 else real + r_term
        imag = i_term if e == 0 else imag + i_term
    return real, imag


def phase_kernel(bits, q_hbm, k_hbm, ev_hbm, rpv_hbm, eig_hbm, w_ref, prod_ref, first_ref, rest_ref, turn_ref, mixer_ref,
                 slabs, lhs, rpv_ref, eig_ref, q_ref, k_ref, ev_ref, sems, small_sems):
    parts, points, slab, modes, pairs = w_ref.shape
    first_slots, per_core = first_ref.shape[:2]
    slots = first_slots + rest_ref.shape[0]
    chunks = modes // ROWS
    pieces = sems.shape[1]

    small = [
        pltpu.make_async_copy(source, target, small_sems.at[at])
        for at, (source, target) in enumerate(
            [(rpv_hbm, rpv_ref), (q_hbm, q_ref), (k_hbm, k_ref), (ev_hbm, ev_ref), (eig_hbm, eig_ref)]
        )
    ]
    for copy in small:
        copy.start()

    def fetch(c, piece):
        some = pl.ds(piece * (points // pieces), points // pieces)
        return pltpu.make_async_copy(
            w_ref.at[:, some, :, pl.ds(c * ROWS, ROWS), :], slabs.at[c, :, some], sems.at[c, piece]
        )

    for c in range(chunks):
        for piece in range(pieces):
            fetch(c, piece).start()
    for copy in small:
        copy.wait()

    me = lax.axis_index("rp")
    core = lax.axis_index("re")
    width = points * ROWS
    spread = (
        lax.broadcasted_iota(jnp.int32, (points, width), 1) // ROWS
        == lax.broadcasted_iota(jnp.int32, (points, width), 0)
    ).astype(jnp.bfloat16)
    vectors = jnp.dot(rpv_ref[...].astype(jnp.bfloat16), spread, preferred_element_type=jnp.float32)
    rows = []
    for offset in sum(slot_offsets(bits), []):
        q = me ^ offset
        row = 0.0
        for axis in range(3):
            row = row + q_ref[axis, q].astype(jnp.float32) * vectors[axis : axis + 1, :]
        rows.append(row)
    angles = wrapped_angle(jnp.concatenate(rows, axis=0))
    cosine, sine = jnp.cos(angles), jnp.sin(angles)
    diagonal = (
        lax.broadcasted_iota(jnp.int32, (ROWS, width), 1) % ROWS
        == lax.broadcasted_iota(jnp.int32, (ROWS, width), 0)
    ).astype(jnp.float32)
    for slot in range(slots):
        cos_block = (cosine[slot : slot + 1] * diagonal).astype(jnp.bfloat16)
        sin_block = (sine[slot : slot + 1] * diagonal).astype(jnp.bfloat16)
        top, bottom = pl.ds(2 * slot * ROWS, ROWS), pl.ds((2 * slot + 1) * ROWS, ROWS)
        lhs[top, :width] = cos_block
        lhs[top, width:] = -sin_block
        lhs[bottom, :width] = sin_block
        lhs[bottom, width:] = cos_block

    k_cos, k_sin = k_phases(core, per_core, slab, k_ref, ev_ref)
    turn_ref[0] = k_cos
    turn_ref[1] = k_sin

    real_vec, imag_vec = eig_ref[0, 0], eig_ref[0, 1]
    rotation = jnp.concatenate(
        [jnp.concatenate([real_vec, imag_vec], axis=1), jnp.concatenate([-imag_vec, real_vec], axis=1)], axis=0
    )
    high = rotation.astype(jnp.bfloat16)
    mixer_ref[0] = high
    mixer_ref[1] = high
    mixer_ref[2] = (rotation - high.astype(jnp.float32)).astype(jnp.bfloat16)

    def send_sum(c):
        for slot in range(slots):
            for i in range(per_core):
                sums = k_sum(prod_ref, c, slot, k_cos, k_sin, per_core + i)
                for part in range(2):
                    place = (i, part, pl.ds(c * ROWS, ROWS), slice(None))
                    if slot < first_slots:
                        first_ref[(slot, *place)] = sums[part].astype(first_ref.dtype)
                    else:
                        rest_ref[(slot - first_slots, *place)] = sums[part].astype(rest_ref.dtype)

    for c in range(chunks):
        if c:
            send_sum(c - 1)
        for piece in range(pieces):
            fetch(c, piece).wait()
        for e in range(slab):
            block = slabs[c, :, :, e].reshape(parts * width, pairs)
            prod_ref[c, e] = jnp.dot(lhs[...], block, preferred_element_type=jnp.float32)
    send_sum(chunks - 1)


def keep_kernel(prod_ref, turn_ref, first_ref, rest_ref):
    first_slots, per_core = first_ref.shape[:2]
    slots = first_slots + rest_ref.shape[0]
    k_cos, k_sin = turn_ref[0], turn_ref[1]
    for c in range(prod_ref.shape[0]):
        for slot in range(slots):
            for i in range(per_core):
                sums = k_sum(prod_ref, c, slot, k_cos, k_sin, i)
                for part in range(2):
                    place = (i, part, pl.ds(c * ROWS, ROWS), slice(None))
                    if slot < first_slots:
                        first_ref[(slot, *place)] = sums[part]
                    else:
                        rest_ref[(slot - first_slots, *place)] = sums[part]


def rotate_kernel(mixer_ref, mine_ref, *refs):
    *got_refs, out_ref = refs
    modes, pairs = mine_ref.shape[-2:]
    mixer = mixer_ref[...].reshape(-1, 2 * modes)
    for i in range(mine_ref.shape[1]):
        source = mine_ref[0, i]
        for got_ref in got_refs:
            source = source + got_ref[0, i].astype(jnp.float32)
        source = source.reshape(2 * modes, pairs)
        high = source.astype(jnp.bfloat16)
        low = (source - high.astype(jnp.float32)).astype(jnp.bfloat16)
        stacked = jnp.concatenate([high, low, high], axis=0)
        turned = lax.dot_general(
            mixer, stacked, (((0,), (0,)), ((), ())), preferred_element_type=jnp.float32
        ).astype(out_ref.dtype)
        out_ref[0, 0, i] = turned[:modes]
        out_ref[0, 1, i] = turned[modes:]


def make_shards(mesh):
    ranks, cores = mesh.shape["rp"], mesh.shape["re"]
    bits = ranks.bit_length() - 1
    vmem = pl.BlockSpec(memory_space=pltpu.VMEM)
    hbm = pl.BlockSpec(memory_space=pltpu.HBM)

    def in_hbm(x):
        return pltpu.with_memory_space_constraint(x, pltpu.HBM)

    def shards(weights, rp_vectors, re_vectors, q_points, k_points, eigvecs):
        parts, points, slab, modes, pairs = weights.shape
        slots = q_points.shape[1]
        per_core = k_points.shape[1] // cores
        chunks = modes // ROWS
        near = near_bits(bits)
        groups, spans = 1 << near, 1 << (bits - near)
        block = (per_core, 2, modes, pairs)
        shapes = [(spans, *block), (slots - spans, *block)]
        pieces = math.gcd(points, PIECES)
        lines = 2 * slots * ROWS
        prod, first_away, rest_away, turn, mixer = pl.pallas_call(
            lambda *refs: phase_kernel(bits, *refs),
            out_shape=(
                jax.ShapeDtypeStruct((chunks, slab, lines, pairs), jnp.float32),
                *[jax.ShapeDtypeStruct(shape, jnp.bfloat16) for shape in shapes],
                jax.ShapeDtypeStruct((2, 2 * per_core, slab), jnp.float32),
                jax.ShapeDtypeStruct((3, 2 * modes, 2 * modes), jnp.bfloat16),
            ),
            in_specs=[hbm] * 6,
            out_specs=(vmem,) * 5,
            scratch_shapes=[
                pltpu.VMEM((chunks, parts, points, slab, ROWS, pairs), jnp.bfloat16),
                pltpu.VMEM((lines, parts * points * ROWS), jnp.bfloat16),
                pltpu.VMEM(rp_vectors.shape, jnp.int32),
                pltpu.VMEM(eigvecs.shape, jnp.float32),
                pltpu.SMEM(q_points.shape, jnp.int32),
                pltpu.SMEM(k_points.shape[::-1], jnp.int32),
                pltpu.SMEM(re_vectors.shape, jnp.int32),
                pltpu.SemaphoreType.DMA((chunks, pieces)),
                pltpu.SemaphoreType.DMA((5,)),
            ],
            compiler_params=pltpu.CompilerParams(vmem_limit_bytes=16 * 2**20),
            name="phase_sums",
        )(*[in_hbm(x) for x in (q_points, k_points.T, re_vectors, rp_vectors, eigvecs, weights)])
        first_sums, rest_sums = pl.pallas_call(
            keep_kernel,
            out_shape=[jax.ShapeDtypeStruct(shape, jnp.float32) for shape in shapes],
            in_specs=[vmem, vmem],
            out_specs=[vmem, vmem],
            compiler_params=pltpu.CompilerParams(vmem_limit_bytes=4 * 2**20),
            cost_estimate=pl.CostEstimate(flops=8 * prod.size, bytes_accessed=4 * prod.size, transcendentals=0),
            name="own_k_sums",
        )(prod, turn)

        def swap(blocks, offset, axis="rp"):
            size = mesh.shape[axis]
            ends = [(r, r ^ offset) for r in range(size)]
            return lax.ppermute(blocks.astype(jnp.bfloat16), axis, ends)

        def wide(blocks):
            return blocks.astype(jnp.float32)

        first_other = swap(first_away, 1, "re")
        rest_other = swap(rest_away, 1, "re")
        last = groups - 1
        first_sums = first_sums + wide(first_other)
        rest_sums = rest_sums + wide(rest_other)
        first_got = swap(first_sums, last)
        width = spans - 1
        beyond = [swap(rest_sums[d * width : (d + 1) * width], d) for d in range(1, last)]
        among = [swap(rest_sums[last * width + d :][:1], d) for d in range(1, last)]
        total = rest_sums[:width] + wide(first_got[:width])
        for got in beyond:
            total = total + wide(got)
        own = rest_sums[last * width :][:1] + wide(first_got[width:])
        half = spans // 2
        while half > 1:
            got = swap(total[half - 1 :], half << near)
            total = total[: half - 1] + wide(got[1:])
            among.append(got[:1])
            half = half // 2
        among.append(swap(total, 1 << near))
        return pl.pallas_call(
            rotate_kernel,
            out_shape=jax.ShapeDtypeStruct((1, 2, per_core, modes, pairs), jnp.bfloat16),
            in_specs=[vmem] * (2 + len(among)),
            out_specs=vmem,
            compiler_params=pltpu.CompilerParams(vmem_limit_bytes=4 * 2**20),
            name="rotate_modes",
        )(mixer, own, *among)

    return shards


def solution(mesh):
    return jax.shard_map(
        make_shards(mesh),
        mesh=mesh,
        in_specs=(
            P(None, "rp", "re", None, None),
            P(None, "rp"),
            P(),
            P(None, "grp"),
            P(None, "grp"),
            P(("grp", "rp"), None, None, None),
        ),
        out_specs=P(("grp", "rp"), None, "re", None, None),
        check_vma=False,
    )
```

```python
import math

import jax
import jax.numpy as jnp
from jax import lax
from jax.experimental import pallas as pl
from jax.experimental.pallas import tpu as pltpu
from jax.sharding import PartitionSpec as P

NFINE = 48
NEAR = 2
PIECES = 2
ROWS = 16


def near_bits(bits):
    return min(NEAR, bits - 1)


def slot_offsets(bits):
    near = near_bits(bits)
    last = (1 << near) - 1
    beyond = [f << near for f in range(1, 1 << (bits - near))]
    return [last | far for far in (*beyond, 0)], [d | far for d in range(last) for far in beyond] + list(range(last))


def wrapped_angle(products):
    turns = jnp.floor((products + 0.5) * (1.0 / NFINE))
    return (products - NFINE * turns) * (2.0 * math.pi / NFINE)


def k_phases(core, per_core, slab, k_ref, ev_ref):
    places = (2 * per_core, slab)
    at_row = lax.broadcasted_iota(jnp.int32, places, 0)
    at_lane = lax.broadcasted_iota(jnp.int32, places, 1)
    products = jnp.zeros(places, jnp.float32)
    for line in range(2 * per_core):
        k = (core ^ (line // per_core)) * per_core + line % per_core
        for e in range(slab):
            total = 0
            for axis in range(3):
                total = total + k_ref[k, axis] * ev_ref[axis, core * slab + e]
            products = jnp.where((at_row == line) & (at_lane == e), total.astype(jnp.float32), products)
    angles = wrapped_angle(products)
    return jnp.cos(angles), jnp.sin(angles)


def k_sum(prod_ref, c, slot, k_cos, k_sin, line):
    slab, _, pairs = prod_ref.shape[1:]
    real = imag = None
    for e in range(slab):
        p_real = prod_ref[c, e, pl.ds(2 * slot * ROWS, ROWS), :]
        p_imag = prod_ref[c, e, pl.ds((2 * slot + 1) * ROWS, ROWS), :]
        cos_e = jnp.broadcast_to(k_cos[line : line + 1, e : e + 1], (ROWS, pairs))
        sin_e = jnp.broadcast_to(k_sin[line : line + 1, e : e + 1], (ROWS, pairs))
        r_term = cos_e * p_real - sin_e * p_imag
        i_term = sin_e * p_real + cos_e * p_imag
        real = r_term if e == 0 else real + r_term
        imag = i_term if e == 0 else imag + i_term
    return real, imag


def phase_kernel(bits, q_hbm, k_hbm, ev_hbm, rpv_hbm, eig_hbm, w_ref, prod_ref, first_ref, rest_ref, turn_ref, mixer_ref,
                 slabs, lhs, rpv_ref, eig_ref, q_ref, k_ref, ev_ref, sems, small_sems):
    parts, points, slab, modes, pairs = w_ref.shape
    first_slots, per_core = first_ref.shape[:2]
    slots = first_slots + rest_ref.shape[0]
    chunks = modes // ROWS
    pieces = sems.shape[1]

    small = [
        pltpu.make_async_copy(source, target, small_sems.at[at])
        for at, (source, target) in enumerate(
            [(rpv_hbm, rpv_ref), (q_hbm, q_ref), (k_hbm, k_ref), (ev_hbm, ev_ref), (eig_hbm, eig_ref)]
        )
    ]
    for copy in small:
        copy.start()

    def fetch(c, piece):
        some = pl.ds(piece * (points // pieces), points // pieces)
        return pltpu.make_async_copy(
            w_ref.at[:, some, :, pl.ds(c * ROWS, ROWS), :], slabs.at[c, :, some], sems.at[c, piece]
        )

    for c in range(chunks):
        for piece in range(pieces):
            fetch(c, piece).start()
    for copy in small:
        copy.wait()

    me = lax.axis_index("rp")
    core = lax.axis_index("re")
    width = points * ROWS
    spread = (
        lax.broadcasted_iota(jnp.int32, (points, width), 1) // ROWS
        == lax.broadcasted_iota(jnp.int32, (points, width), 0)
    ).astype(jnp.bfloat16)
    vectors = jnp.dot(rpv_ref[...].astype(jnp.bfloat16), spread, preferred_element_type=jnp.float32)
    rows = []
    for offset in sum(slot_offsets(bits), []):
        q = me ^ offset
        row = 0.0
        for axis in range(3):
            row = row + q_ref[axis, q].astype(jnp.float32) * vectors[axis : axis + 1, :]
        rows.append(row)
    angles = wrapped_angle(jnp.concatenate(rows, axis=0))
    cosine, sine = jnp.cos(angles), jnp.sin(angles)
    diagonal = (
        lax.broadcasted_iota(jnp.int32, (ROWS, width), 1) % ROWS
        == lax.broadcasted_iota(jnp.int32, (ROWS, width), 0)
    ).astype(jnp.float32)
    for slot in range(slots):
        cos_block = (cosine[slot : slot + 1] * diagonal).astype(jnp.bfloat16)
        sin_block = (sine[slot : slot + 1] * diagonal).astype(jnp.bfloat16)
        top, bottom = pl.ds(2 * slot * ROWS, ROWS), pl.ds((2 * slot + 1) * ROWS, ROWS)
        lhs[top, :width] = cos_block
        lhs[top, width:] = -sin_block
        lhs[bottom, :width] = sin_block
        lhs[bottom, width:] = cos_block

    k_cos, k_sin = k_phases(core, per_core, slab, k_ref, ev_ref)
    turn_ref[0] = k_cos
    turn_ref[1] = k_sin

    real_vec, imag_vec = eig_ref[0, 0], eig_ref[0, 1]
    rotation = jnp.concatenate(
        [jnp.concatenate([real_vec, imag_vec], axis=1), jnp.concatenate([-imag_vec, real_vec], axis=1)], axis=0
    )
    high = rotation.astype(jnp.bfloat16)
    mixer_ref[0] = high
    mixer_ref[1] = high
    mixer_ref[2] = (rotation - high.astype(jnp.float32)).astype(jnp.bfloat16)

    def send_sum(c):
        for slot in range(slots):
            for i in range(per_core):
                sums = k_sum(prod_ref, c, slot, k_cos, k_sin, per_core + i)
                for part in range(2):
                    place = (i, part, pl.ds(c * ROWS, ROWS), slice(None))
                    if slot < first_slots:
                        first_ref[(slot, *place)] = sums[part].astype(first_ref.dtype)
                    else:
                        rest_ref[(slot - first_slots, *place)] = sums[part].astype(rest_ref.dtype)

    for c in range(chunks):
        if c:
            send_sum(c - 1)
        for piece in range(pieces):
            fetch(c, piece).wait()
        for e in range(slab):
            block = slabs[c, :, :, e].reshape(parts * width, pairs)
            prod_ref[c, e] = jnp.dot(lhs[...], block, preferred_element_type=jnp.float32)
    send_sum(chunks - 1)


def keep_kernel(prod_ref, turn_ref, first_ref, rest_ref):
    first_slots, per_core = first_ref.shape[:2]
    slots = first_slots + rest_ref.shape[0]
    k_cos, k_sin = turn_ref[0], turn_ref[1]
    for c in range(prod_ref.shape[0]):
        for slot in range(slots):
            for i in range(per_core):
                sums = k_sum(prod_ref, c, slot, k_cos, k_sin, i)
                for part in range(2):
                    place = (i, part, pl.ds(c * ROWS, ROWS), slice(None))
                    if slot < first_slots:
                        first_ref[(slot, *place)] = sums[part]
                    else:
                        rest_ref[(slot - first_slots, *place)] = sums[part]


def turn_by(mixer, source):
    return lax.dot_general(mixer, source, (((0,), (0,)), ((), ())), preferred_element_type=jnp.float32)


def early_kernel(mixer_ref, mine_ref, *refs):
    *got_refs, out_ref = refs
    modes, pairs = mine_ref.shape[-2:]
    mixer = mixer_ref[...].reshape(-1, 2 * modes)
    for i in range(mine_ref.shape[1]):
        source = mine_ref[0, i]
        for got_ref in got_refs:
            source = source + got_ref[0, i].astype(jnp.float32)
        source = source.reshape(2 * modes, pairs)
        high = source.astype(jnp.bfloat16)
        low = (source - high.astype(jnp.float32)).astype(jnp.bfloat16)
        out_ref[i] = turn_by(mixer, jnp.concatenate([high, low, high], axis=0))


def late_kernel(mixer_ref, early_ref, got_ref, out_ref):
    modes, pairs = got_ref.shape[-2:]
    mixer = mixer_ref[1:].reshape(-1, 2 * modes)
    for i in range(got_ref.shape[1]):
        got = got_ref[0, i].reshape(2 * modes, pairs)
        turned = (early_ref[i] + turn_by(mixer, jnp.concatenate([got, got], axis=0))).astype(out_ref.dtype)
        out_ref[0, 0, i] = turned[:modes]
        out_ref[0, 1, i] = turned[modes:]


def make_shards(mesh):
    ranks, cores = mesh.shape["rp"], mesh.shape["re"]
    bits = ranks.bit_length() - 1
    vmem = pl.BlockSpec(memory_space=pltpu.VMEM)
    hbm = pl.BlockSpec(memory_space=pltpu.HBM)

    def in_hbm(x):
        return pltpu.with_memory_space_constraint(x, pltpu.HBM)

    def shards(weights, rp_vectors, re_vectors, q_points, k_points, eigvecs):
        parts, points, slab, modes, pairs = weights.shape
        slots = q_points.shape[1]
        per_core = k_points.shape[1] // cores
        chunks = modes // ROWS
        near = near_bits(bits)
        groups, spans = 1 << near, 1 << (bits - near)
        block = (per_core, 2, modes, pairs)
        shapes = [(spans, *block), (slots - spans, *block)]
        pieces = math.gcd(points, PIECES)
        lines = 2 * slots * ROWS
        prod, first_away, rest_away, turn, mixer = pl.pallas_call(
            lambda *refs: phase_kernel(bits, *refs),
            out_shape=(
                jax.ShapeDtypeStruct((chunks, slab, lines, pairs), jnp.float32),
                *[jax.ShapeDtypeStruct(shape, jnp.bfloat16) for shape in shapes],
                jax.ShapeDtypeStruct((2, 2 * per_core, slab), jnp.float32),
                jax.ShapeDtypeStruct((3, 2 * modes, 2 * modes), jnp.bfloat16),
            ),
            in_specs=[hbm] * 6,
            out_specs=(vmem,) * 5,
            scratch_shapes=[
                pltpu.VMEM((chunks, parts, points, slab, ROWS, pairs), jnp.bfloat16),
                pltpu.VMEM((lines, parts * points * ROWS), jnp.bfloat16),
                pltpu.VMEM(rp_vectors.shape, jnp.int32),
                pltpu.VMEM(eigvecs.shape, jnp.float32),
                pltpu.SMEM(q_points.shape, jnp.int32),
                pltpu.SMEM(k_points.shape[::-1], jnp.int32),
                pltpu.SMEM(re_vectors.shape, jnp.int32),
                pltpu.SemaphoreType.DMA((chunks, pieces)),
                pltpu.SemaphoreType.DMA((5,)),
            ],
            compiler_params=pltpu.CompilerParams(vmem_limit_bytes=16 * 2**20),
            name="phase_sums",
        )(*[in_hbm(x) for x in (q_points, k_points.T, re_vectors, rp_vectors, eigvecs, weights)])
        first_sums, rest_sums = pl.pallas_call(
            keep_kernel,
            out_shape=[jax.ShapeDtypeStruct(shape, jnp.float32) for shape in shapes],
            in_specs=[vmem, vmem],
            out_specs=[vmem, vmem],
            compiler_params=pltpu.CompilerParams(vmem_limit_bytes=4 * 2**20),
            cost_estimate=pl.CostEstimate(flops=8 * prod.size, bytes_accessed=4 * prod.size, transcendentals=0),
            name="own_k_sums",
        )(prod, turn)

        def swap(blocks, offset, axis="rp"):
            size = mesh.shape[axis]
            ends = [(r, r ^ offset) for r in range(size)]
            return lax.ppermute(blocks.astype(jnp.bfloat16), axis, ends)

        def wide(blocks):
            return blocks.astype(jnp.float32)

        first_other = swap(first_away, 1, "re")
        rest_other = swap(rest_away, 1, "re")
        last = groups - 1
        first_sums = first_sums + wide(first_other)
        rest_sums = rest_sums + wide(rest_other)
        first_got = swap(first_sums, last)
        width = spans - 1
        beyond = [swap(rest_sums[d * width : (d + 1) * width], d) for d in reversed(range(1, last))]
        among = [swap(rest_sums[last * width + d :][:1], d) for d in reversed(range(1, last))]
        total = rest_sums[:width] + wide(first_got[:width])
        for got in beyond:
            total = total + wide(got)
        own = rest_sums[last * width :][:1] + wide(first_got[width:])
        half = spans // 2
        while half > 1:
            got = swap(total[half - 1 :], half << near)
            total = total[: half - 1] + wide(got[1:])
            among.append(got[:1])
            half = half // 2
        across = swap(total, 1 << near)
        early = pl.pallas_call(
            early_kernel,
            out_shape=jax.ShapeDtypeStruct((per_core, 2 * modes, pairs), jnp.float32),
            in_specs=[vmem] * (2 + len(among)),
            out_specs=vmem,
            compiler_params=pltpu.CompilerParams(vmem_limit_bytes=4 * 2**20),
            cost_estimate=pl.CostEstimate(
                flops=2 * mixer.size * per_core * pairs, bytes_accessed=16 * per_core * modes * pairs, transcendentals=0
            ),
            name="rotate_early",
        )(mixer, own, *among)
        return pl.pallas_call(
            late_kernel,
            out_shape=jax.ShapeDtypeStruct((1, 2, per_core, modes, pairs), jnp.bfloat16),
            in_specs=[vmem] * 3,
            out_specs=vmem,
            compiler_params=pltpu.CompilerParams(vmem_limit_bytes=4 * 2**20),
            name="rotate_last",
        )(mixer, early, across)

    return shards


def solution(mesh):
    return jax.shard_map(
        make_shards(mesh),
        mesh=mesh,
        in_specs=(
            P(None, "rp", "re", None, None),
            P(None, "rp"),
            P(),
            P(None, "grp"),
            P(None, "grp"),
            P(("grp", "rp"), None, None, None),
        ),
        out_specs=P(("grp", "rp"), None, "re", None, None),
        check_vma=False,
    )
```

```python
import math

import jax
import jax.numpy as jnp
from jax import lax
from jax.experimental import pallas as pl
from jax.experimental.pallas import tpu as pltpu
from jax.sharding import PartitionSpec as P

NFINE = 48
NEAR = 2
PIECES = 2
ROWS = 16


def near_bits(bits):
    return min(NEAR, bits - 1)


def slot_offsets(bits):
    near = near_bits(bits)
    last = (1 << near) - 1
    beyond = [f << near for f in range(1, 1 << (bits - near))]
    return [last | far for far in (*beyond, 0)], [d | far for d in range(last) for far in beyond] + list(range(last))


def wrapped_angle(products):
    turns = jnp.floor((products + 0.5) * (1.0 / NFINE))
    return (products - NFINE * turns) * (2.0 * math.pi / NFINE)


def k_phases(core, per_core, slab, k_ref, ev_ref):
    places = (2 * per_core, slab)
    at_row = lax.broadcasted_iota(jnp.int32, places, 0)
    at_lane = lax.broadcasted_iota(jnp.int32, places, 1)
    products = jnp.zeros(places, jnp.float32)
    for line in range(2 * per_core):
        k = (core ^ (line // per_core)) * per_core + line % per_core
        for e in range(slab):
            total = 0
            for axis in range(3):
                total = total + k_ref[k, axis] * ev_ref[axis, core * slab + e]
            products = jnp.where((at_row == line) & (at_lane == e), total.astype(jnp.float32), products)
    angles = wrapped_angle(products)
    return jnp.cos(angles), jnp.sin(angles)


def k_sum(prod_ref, c, slot, k_cos, k_sin, line):
    slab, _, pairs = prod_ref.shape[1:]
    real = imag = None
    for e in range(slab):
        p_real = prod_ref[c, e, pl.ds(2 * slot * ROWS, ROWS), :]
        p_imag = prod_ref[c, e, pl.ds((2 * slot + 1) * ROWS, ROWS), :]
        cos_e = jnp.broadcast_to(k_cos[line : line + 1, e : e + 1], (ROWS, pairs))
        sin_e = jnp.broadcast_to(k_sin[line : line + 1, e : e + 1], (ROWS, pairs))
        r_term = cos_e * p_real - sin_e * p_imag
        i_term = sin_e * p_real + cos_e * p_imag
        real = r_term if e == 0 else real + r_term
        imag = i_term if e == 0 else imag + i_term
    return real, imag


def phase_kernel(bits, q_hbm, k_hbm, ev_hbm, rpv_hbm, eig_hbm, w_ref, prod_ref, first_ref, rest_ref, turn_ref, mixer_ref,
                 slabs, lhs, rpv_ref, eig_ref, q_ref, k_ref, ev_ref, sems, small_sems):
    parts, points, slab, modes, pairs = w_ref.shape
    first_slots, per_core = first_ref.shape[:2]
    slots = first_slots + rest_ref.shape[0]
    chunks = modes // ROWS
    pieces = sems.shape[1]

    small = [
        pltpu.make_async_copy(source, target, small_sems.at[at])
        for at, (source, target) in enumerate(
            [(rpv_hbm, rpv_ref), (q_hbm, q_ref), (k_hbm, k_ref), (ev_hbm, ev_ref), (eig_hbm, eig_ref)]
        )
    ]
    for copy in small:
        copy.start()

    def fetch(c, piece):
        some = pl.ds(piece * (points // pieces), points // pieces)
        return pltpu.make_async_copy(
            w_ref.at[:, some, :, pl.ds(c * ROWS, ROWS), :], slabs.at[c, :, some], sems.at[c, piece]
        )

    for c in range(chunks):
        for piece in range(pieces):
            fetch(c, piece).start()
    for copy in small:
        copy.wait()

    me = lax.axis_index("rp")
    core = lax.axis_index("re")
    width = points * ROWS
    spread = (
        lax.broadcasted_iota(jnp.int32, (points, width), 1) // ROWS
        == lax.broadcasted_iota(jnp.int32, (points, width), 0)
    ).astype(jnp.bfloat16)
    vectors = jnp.dot(rpv_ref[...].astype(jnp.bfloat16), spread, preferred_element_type=jnp.float32)
    rows = []
    for offset in sum(slot_offsets(bits), []):
        q = me ^ offset
        row = 0.0
        for axis in range(3):
            row = row + q_ref[axis, q].astype(jnp.float32) * vectors[axis : axis + 1, :]
        rows.append(row)
    angles = wrapped_angle(jnp.concatenate(rows, axis=0))
    cosine, sine = jnp.cos(angles), jnp.sin(angles)
    diagonal = (
        lax.broadcasted_iota(jnp.int32, (ROWS, width), 1) % ROWS
        == lax.broadcasted_iota(jnp.int32, (ROWS, width), 0)
    ).astype(jnp.float32)
    for slot in range(slots):
        cos_block = (cosine[slot : slot + 1] * diagonal).astype(jnp.bfloat16)
        sin_block = (sine[slot : slot + 1] * diagonal).astype(jnp.bfloat16)
        top, bottom = pl.ds(2 * slot * ROWS, ROWS), pl.ds((2 * slot + 1) * ROWS, ROWS)
        lhs[top, :width] = cos_block
        lhs[top, width:] = -sin_block
        lhs[bottom, :width] = sin_block
        lhs[bottom, width:] = cos_block

    k_cos, k_sin = k_phases(core, per_core, slab, k_ref, ev_ref)
    turn_ref[0] = k_cos
    turn_ref[1] = k_sin

    real_vec, imag_vec = eig_ref[0, 0], eig_ref[0, 1]
    rotation = jnp.concatenate(
        [jnp.concatenate([real_vec, imag_vec], axis=1), jnp.concatenate([-imag_vec, real_vec], axis=1)], axis=0
    )
    turned = rotation.T
    high = turned.astype(jnp.bfloat16)
    low = (turned - high.astype(jnp.float32)).astype(jnp.bfloat16)
    mixer_ref[...] = jnp.concatenate([high, low, high], axis=1)

    def send_sum(c):
        for slot in range(slots):
            for i in range(per_core):
                sums = k_sum(prod_ref, c, slot, k_cos, k_sin, per_core + i)
                for part in range(2):
                    place = (i, part, pl.ds(c * ROWS, ROWS), slice(None))
                    if slot < first_slots:
                        first_ref[(slot, *place)] = sums[part].astype(first_ref.dtype)
                    else:
                        rest_ref[(slot - first_slots, *place)] = sums[part].astype(rest_ref.dtype)

    for c in range(chunks):
        if c:
            send_sum(c - 1)
        for piece in range(pieces):
            fetch(c, piece).wait()
        for e in range(slab):
            block = slabs[c, :, :, e].reshape(parts * width, pairs)
            prod_ref[c, e] = jnp.dot(lhs[...], block, preferred_element_type=jnp.float32)
    send_sum(chunks - 1)


def keep_kernel(prod_ref, turn_ref, first_ref, rest_ref):
    first_slots, per_core = first_ref.shape[:2]
    slots = first_slots + rest_ref.shape[0]
    k_cos, k_sin = turn_ref[0], turn_ref[1]
    for c in range(prod_ref.shape[0]):
        for slot in range(slots):
            for i in range(per_core):
                sums = k_sum(prod_ref, c, slot, k_cos, k_sin, i)
                for part in range(2):
                    place = (i, part, pl.ds(c * ROWS, ROWS), slice(None))
                    if slot < first_slots:
                        first_ref[(slot, *place)] = sums[part]
                    else:
                        rest_ref[(slot - first_slots, *place)] = sums[part]


def early_kernel(mixer_ref, mine_ref, *refs):
    *got_refs, out_ref = refs
    modes, pairs = mine_ref.shape[-2:]
    mixer = mixer_ref[...]
    for i in range(mine_ref.shape[1]):
        source = mine_ref[0, i]
        for got_ref in got_refs:
            source = source + got_ref[0, i].astype(jnp.float32)
        source = source.reshape(2 * modes, pairs)
        high = source.astype(jnp.bfloat16)
        low = (source - high.astype(jnp.float32)).astype(jnp.bfloat16)
        stacked = jnp.concatenate([high, high, low], axis=0)
        out_ref[i] = jnp.dot(mixer, stacked, preferred_element_type=jnp.float32)


def late_kernel(mixer_ref, early_ref, got_ref, out_ref):
    modes, pairs = got_ref.shape[-2:]
    mixer = mixer_ref[:, : 4 * modes]
    for i in range(got_ref.shape[1]):
        got = got_ref[0, i].reshape(2 * modes, pairs)
        turned = jnp.dot(mixer, jnp.concatenate([got, got], axis=0), preferred_element_type=jnp.float32)
        turned = (early_ref[i] + turned).astype(out_ref.dtype)
        out_ref[0, 0, i] = turned[:modes]
        out_ref[0, 1, i] = turned[modes:]


def make_shards(mesh):
    ranks, cores = mesh.shape["rp"], mesh.shape["re"]
    bits = ranks.bit_length() - 1
    vmem = pl.BlockSpec(memory_space=pltpu.VMEM)
    hbm = pl.BlockSpec(memory_space=pltpu.HBM)

    def in_hbm(x):
        return pltpu.with_memory_space_constraint(x, pltpu.HBM)

    def shards(weights, rp_vectors, re_vectors, q_points, k_points, eigvecs):
        parts, points, slab, modes, pairs = weights.shape
        slots = q_points.shape[1]
        per_core = k_points.shape[1] // cores
        chunks = modes // ROWS
        near = near_bits(bits)
        groups, spans = 1 << near, 1 << (bits - near)
        block = (per_core, 2, modes, pairs)
        shapes = [(spans, *block), (slots - spans, *block)]
        pieces = math.gcd(points, PIECES)
        lines = 2 * slots * ROWS
        prod, first_away, rest_away, turn, mixer = pl.pallas_call(
            lambda *refs: phase_kernel(bits, *refs),
            out_shape=(
                jax.ShapeDtypeStruct((chunks, slab, lines, pairs), jnp.float32),
                *[jax.ShapeDtypeStruct(shape, jnp.bfloat16) for shape in shapes],
                jax.ShapeDtypeStruct((2, 2 * per_core, slab), jnp.float32),
                jax.ShapeDtypeStruct((2 * modes, 6 * modes), jnp.bfloat16),
            ),
            in_specs=[hbm] * 6,
            out_specs=(vmem,) * 5,
            scratch_shapes=[
                pltpu.VMEM((chunks, parts, points, slab, ROWS, pairs), jnp.bfloat16),
                pltpu.VMEM((lines, parts * points * ROWS), jnp.bfloat16),
                pltpu.VMEM(rp_vectors.shape, jnp.int32),
                pltpu.VMEM(eigvecs.shape, jnp.float32),
                pltpu.SMEM(q_points.shape, jnp.int32),
                pltpu.SMEM(k_points.shape[::-1], jnp.int32),
                pltpu.SMEM(re_vectors.shape, jnp.int32),
                pltpu.SemaphoreType.DMA((chunks, pieces)),
                pltpu.SemaphoreType.DMA((5,)),
            ],
            compiler_params=pltpu.CompilerParams(vmem_limit_bytes=16 * 2**20),
            name="phase_sums",
        )(*[in_hbm(x) for x in (q_points, k_points.T, re_vectors, rp_vectors, eigvecs, weights)])
        first_sums, rest_sums = pl.pallas_call(
            keep_kernel,
            out_shape=[jax.ShapeDtypeStruct(shape, jnp.float32) for shape in shapes],
            in_specs=[vmem, vmem],
            out_specs=[vmem, vmem],
            compiler_params=pltpu.CompilerParams(vmem_limit_bytes=4 * 2**20),
            cost_estimate=pl.CostEstimate(flops=8 * prod.size, bytes_accessed=4 * prod.size, transcendentals=0),
            name="own_k_sums",
        )(prod, turn)

        def swap(blocks, offset, axis="rp"):
            size = mesh.shape[axis]
            ends = [(r, r ^ offset) for r in range(size)]
            return lax.ppermute(blocks.astype(jnp.bfloat16), axis, ends)

        def wide(blocks):
            return blocks.astype(jnp.float32)

        first_other = swap(first_away, 1, "re")
        rest_other = swap(rest_away, 1, "re")
        last = groups - 1
        first_sums = first_sums + wide(first_other)
        rest_sums = rest_sums + wide(rest_other)
        first_got = swap(first_sums, last)
        width = spans - 1
        beyond = [swap(rest_sums[d * width : (d + 1) * width], d) for d in reversed(range(1, last))]
        among = [swap(rest_sums[last * width + d :][:1], d) for d in reversed(range(1, last))]
        total = rest_sums[:width] + wide(first_got[:width])
        for got in beyond:
            total = total + wide(got)
        own = rest_sums[last * width :][:1] + wide(first_got[width:])
        half = spans // 2
        while half > 1:
            got = swap(total[half - 1 :], half << near)
            total = total[: half - 1] + wide(got[1:])
            among.append(got[:1])
            half = half // 2
        across = swap(total, 1 << near)
        early = pl.pallas_call(
            early_kernel,
            out_shape=jax.ShapeDtypeStruct((per_core, 2 * modes, pairs), jnp.float32),
            in_specs=[vmem] * (2 + len(among)),
            out_specs=vmem,
            compiler_params=pltpu.CompilerParams(vmem_limit_bytes=4 * 2**20),
            cost_estimate=pl.CostEstimate(
                flops=2 * mixer.size * per_core * pairs, bytes_accessed=16 * per_core * modes * pairs, transcendentals=0
            ),
            name="rotate_early",
        )(mixer, own, *among)
        return pl.pallas_call(
            late_kernel,
            out_shape=jax.ShapeDtypeStruct((1, 2, per_core, modes, pairs), jnp.bfloat16),
            in_specs=[vmem] * 3,
            out_specs=vmem,
            compiler_params=pltpu.CompilerParams(vmem_limit_bytes=4 * 2**20),
            name="rotate_last",
        )(mixer, early, across)

    return shards


def solution(mesh):
    return jax.shard_map(
        make_shards(mesh),
        mesh=mesh,
        in_specs=(
            P(None, "rp", "re", None, None),
            P(None, "rp"),
            P(),
            P(None, "grp"),
            P(None, "grp"),
            P(("grp", "rp"), None, None, None),
        ),
        out_specs=P(("grp", "rp"), None, "re", None, None),
        check_vma=False,
    )
```

```python
import math

import jax
import jax.numpy as jnp
from jax import lax
from jax.experimental import pallas as pl
from jax.experimental.pallas import tpu as pltpu
from jax.sharding import PartitionSpec as P

NFINE = 48
NEAR = 2
PIECES = 2
ROWS = 16


def near_bits(bits):
    return min(NEAR, bits - 1)


def slot_offsets(bits):
    near = near_bits(bits)
    last = (1 << near) - 1
    beyond = [f << near for f in range(1, 1 << (bits - near))]
    return [last | far for far in (*beyond, 0)], [d | far for d in range(last) for far in beyond] + list(range(last))


def wrapped_angle(products):
    turns = jnp.floor((products + 0.5) * (1.0 / NFINE))
    return (products - NFINE * turns) * (2.0 * math.pi / NFINE)


def k_phases(core, per_core, slab, k_ref, ev_ref):
    places = (2 * per_core, slab)
    at_row = lax.broadcasted_iota(jnp.int32, places, 0)
    at_lane = lax.broadcasted_iota(jnp.int32, places, 1)
    products = jnp.zeros(places, jnp.float32)
    for line in range(2 * per_core):
        k = (core ^ (line // per_core)) * per_core + line % per_core
        for e in range(slab):
            total = 0
            for axis in range(3):
                total = total + k_ref[k, axis] * ev_ref[axis, core * slab + e]
            products = jnp.where((at_row == line) & (at_lane == e), total.astype(jnp.float32), products)
    angles = wrapped_angle(products)
    return jnp.cos(angles), jnp.sin(angles)


def k_sum(prod_ref, c, slot, k_cos, k_sin, line):
    slab, _, pairs = prod_ref.shape[1:]
    real = imag = None
    for e in range(slab):
        p_real = prod_ref[c, e, pl.ds(2 * slot * ROWS, ROWS), :]
        p_imag = prod_ref[c, e, pl.ds((2 * slot + 1) * ROWS, ROWS), :]
        cos_e = jnp.broadcast_to(k_cos[line : line + 1, e : e + 1], (ROWS, pairs))
        sin_e = jnp.broadcast_to(k_sin[line : line + 1, e : e + 1], (ROWS, pairs))
        r_term = cos_e * p_real - sin_e * p_imag
        i_term = sin_e * p_real + cos_e * p_imag
        real = r_term if e == 0 else real + r_term
        imag = i_term if e == 0 else imag + i_term
    return real, imag


def phase_kernel(bits, q_hbm, k_hbm, ev_hbm, rpv_hbm, eig_hbm, w_ref, prod_ref, first_ref, rest_ref, turn_ref, mixer_ref,
                 slabs, lhs, rpv_ref, eig_ref, q_ref, k_ref, ev_ref, sems, small_sems):
    parts, points, slab, modes, pairs = w_ref.shape
    first_slots, per_core = first_ref.shape[:2]
    slots = first_slots + rest_ref.shape[0]
    chunks = modes // ROWS
    pieces = sems.shape[1]

    small = [
        pltpu.make_async_copy(source, target, small_sems.at[at])
        for at, (source, target) in enumerate(
            [(rpv_hbm, rpv_ref), (q_hbm, q_ref), (k_hbm, k_ref), (ev_hbm, ev_ref), (eig_hbm, eig_ref)]
        )
    ]
    for copy in small:
        copy.start()

    def fetch(c, piece):
        some = pl.ds(piece * (points // pieces), points // pieces)
        return pltpu.make_async_copy(
            w_ref.at[:, some, :, pl.ds(c * ROWS, ROWS), :], slabs.at[c, :, some], sems.at[c, piece]
        )

    for c in range(chunks):
        for piece in range(pieces):
            fetch(c, piece).start()
    for copy in small:
        copy.wait()

    me = lax.axis_index("rp")
    core = lax.axis_index("re")
    width = points * ROWS
    spread = (
        lax.broadcasted_iota(jnp.int32, (points, width), 1) // ROWS
        == lax.broadcasted_iota(jnp.int32, (points, width), 0)
    ).astype(jnp.bfloat16)
    vectors = jnp.dot(rpv_ref[...].astype(jnp.bfloat16), spread, preferred_element_type=jnp.float32)
    rows = []
    for offset in sum(slot_offsets(bits), []):
        q = me ^ offset
        row = 0.0
        for axis in range(3):
            row = row + q_ref[axis, q].astype(jnp.float32) * vectors[axis : axis + 1, :]
        rows.append(row)
    angles = wrapped_angle(jnp.concatenate(rows, axis=0))
    cosine, sine = jnp.cos(angles), jnp.sin(angles)
    diagonal = (
        lax.broadcasted_iota(jnp.int32, (ROWS, width), 1) % ROWS
        == lax.broadcasted_iota(jnp.int32, (ROWS, width), 0)
    ).astype(jnp.float32)
    for slot in range(slots):
        cos_block = (cosine[slot : slot + 1] * diagonal).astype(jnp.bfloat16)
        sin_block = (sine[slot : slot + 1] * diagonal).astype(jnp.bfloat16)
        top, bottom = pl.ds(2 * slot * ROWS, ROWS), pl.ds((2 * slot + 1) * ROWS, ROWS)
        lhs[top, :width] = cos_block
        lhs[top, width:] = -sin_block
        lhs[bottom, :width] = sin_block
        lhs[bottom, width:] = cos_block

    k_cos, k_sin = k_phases(core, per_core, slab, k_ref, ev_ref)
    turn_ref[0] = k_cos
    turn_ref[1] = k_sin

    real_vec, imag_vec = eig_ref[0, 0], eig_ref[0, 1]
    rotation = jnp.concatenate(
        [jnp.concatenate([real_vec, imag_vec], axis=1), jnp.concatenate([-imag_vec, real_vec], axis=1)], axis=0
    )
    turned = rotation.T
    high = turned.astype(jnp.bfloat16)
    low = (turned - high.astype(jnp.float32)).astype(jnp.bfloat16)
    mixer_ref[...] = jnp.concatenate([high, low, high], axis=1)

    def send_sum(c):
        for slot in range(slots):
            for i in range(per_core):
                sums = k_sum(prod_ref, c, slot, k_cos, k_sin, per_core + i)
                for part in range(2):
                    place = (i, part, pl.ds(c * ROWS, ROWS), slice(None))
                    if slot < first_slots:
                        first_ref[(slot, *place)] = sums[part].astype(first_ref.dtype)
                    else:
                        rest_ref[(slot - first_slots, *place)] = sums[part].astype(rest_ref.dtype)

    for c in range(chunks):
        if c:
            send_sum(c - 1)
        for piece in range(pieces):
            fetch(c, piece).wait()
        for e in range(slab):
            block = slabs[c, :, :, e].reshape(parts * width, pairs)
            prod_ref[c, e] = jnp.dot(lhs[...], block, preferred_element_type=jnp.float32)
    send_sum(chunks - 1)


def keep_kernel(prod_ref, turn_ref, first_ref, rest_ref):
    first_slots, per_core = first_ref.shape[:2]
    slots = first_slots + rest_ref.shape[0]
    k_cos, k_sin = turn_ref[0], turn_ref[1]
    for c in range(prod_ref.shape[0]):
        for slot in range(slots):
            for i in range(per_core):
                sums = k_sum(prod_ref, c, slot, k_cos, k_sin, i)
                for part in range(2):
                    place = (i, part, pl.ds(c * ROWS, ROWS), slice(None))
                    if slot < first_slots:
                        first_ref[(slot, *place)] = sums[part]
                    else:
                        rest_ref[(slot - first_slots, *place)] = sums[part]


def early_kernel(mixer_ref, mine_ref, *refs):
    *got_refs, out_ref = refs
    modes, pairs = mine_ref.shape[-2:]
    mixer = mixer_ref[...]
    for i in range(mine_ref.shape[1]):
        source = mine_ref[0, i]
        for got_ref in got_refs:
            source = source + got_ref[0, i].astype(jnp.float32)
        source = source.reshape(2 * modes, pairs)
        high = source.astype(jnp.bfloat16)
        low = (source - high.astype(jnp.float32)).astype(jnp.bfloat16)
        stacked = jnp.concatenate([high, high, low], axis=0)
        out_ref[i] = jnp.dot(mixer, stacked, preferred_element_type=jnp.float32)


def late_kernel(mixer_ref, early_ref, got_ref, out_ref):
    modes, pairs = got_ref.shape[-2:]
    mixer = mixer_ref[:, : 4 * modes]
    for i in range(got_ref.shape[1]):
        got = got_ref[0, i].reshape(2 * modes, pairs)
        turned = jnp.dot(mixer, jnp.concatenate([got, got], axis=0), preferred_element_type=jnp.float32)
        turned = (early_ref[i] + turned).astype(out_ref.dtype)
        out_ref[0, 0, i] = turned[:modes]
        out_ref[0, 1, i] = turned[modes:]


def make_shards(mesh):
    ranks, cores = mesh.shape["rp"], mesh.shape["re"]
    bits = ranks.bit_length() - 1
    vmem = pl.BlockSpec(memory_space=pltpu.VMEM)
    hbm = pl.BlockSpec(memory_space=pltpu.HBM)

    def in_hbm(x):
        return pltpu.with_memory_space_constraint(x, pltpu.HBM)

    def shards(weights, rp_vectors, re_vectors, q_points, k_points, eigvecs):
        parts, points, slab, modes, pairs = weights.shape
        slots = q_points.shape[1]
        per_core = k_points.shape[1] // cores
        chunks = modes // ROWS
        near = near_bits(bits)
        groups, spans = 1 << near, 1 << (bits - near)
        block = (per_core, 2, modes, pairs)
        shapes = [(spans, *block), (slots - spans, *block)]
        pieces = math.gcd(points, PIECES)
        lines = 2 * slots * ROWS
        prod, first_away, rest_away, turn, mixer = pl.pallas_call(
            lambda *refs: phase_kernel(bits, *refs),
            out_shape=(
                jax.ShapeDtypeStruct((chunks, slab, lines, pairs), jnp.float32),
                *[jax.ShapeDtypeStruct(shape, jnp.bfloat16) for shape in shapes],
                jax.ShapeDtypeStruct((2, 2 * per_core, slab), jnp.float32),
                jax.ShapeDtypeStruct((2 * modes, 6 * modes), jnp.bfloat16),
            ),
            in_specs=[hbm] * 6,
            out_specs=(vmem,) * 5,
            scratch_shapes=[
                pltpu.VMEM((chunks, parts, points, slab, ROWS, pairs), jnp.bfloat16),
                pltpu.VMEM((lines, parts * points * ROWS), jnp.bfloat16),
                pltpu.VMEM(rp_vectors.shape, jnp.int32),
                pltpu.VMEM(eigvecs.shape, jnp.float32),
                pltpu.SMEM(q_points.shape, jnp.int32),
                pltpu.SMEM(k_points.shape[::-1], jnp.int32),
                pltpu.SMEM(re_vectors.shape, jnp.int32),
                pltpu.SemaphoreType.DMA((chunks, pieces)),
                pltpu.SemaphoreType.DMA((5,)),
            ],
            compiler_params=pltpu.CompilerParams(vmem_limit_bytes=16 * 2**20),
            name="phase_sums",
        )(*[in_hbm(x) for x in (q_points, k_points.T, re_vectors, rp_vectors, eigvecs, weights)])
        first_sums, rest_sums = pl.pallas_call(
            keep_kernel,
            out_shape=[jax.ShapeDtypeStruct(shape, jnp.float32) for shape in shapes],
            in_specs=[vmem, vmem],
            out_specs=[vmem, vmem],
            compiler_params=pltpu.CompilerParams(vmem_limit_bytes=4 * 2**20),
            cost_estimate=pl.CostEstimate(flops=8 * prod.size, bytes_accessed=4 * prod.size, transcendentals=0),
            name="own_k_sums",
        )(prod, turn)

        def swap(blocks, offset, axis="rp"):
            size = mesh.shape[axis]
            ends = [(r, r ^ offset) for r in range(size)]
            return lax.ppermute(blocks.astype(jnp.bfloat16), axis, ends)

        def wide(blocks):
            return blocks.astype(jnp.float32)

        first_other = swap(first_away, 1, "re")
        rest_other = swap(rest_away, 1, "re")
        last = groups - 1
        first_sums = first_sums + wide(first_other)
        rest_sums = rest_sums + wide(rest_other)
        first_got = swap(first_sums, last)
        width = spans - 1
        beyond = [swap(rest_sums[d * width : (d + 1) * width], d) for d in range(1, last)]
        among = [swap(rest_sums[last * width + d :][:1], d) for d in range(1, last)]
        total = rest_sums[:width] + wide(first_got[:width])
        for got in beyond:
            total = total + wide(got)
        own = rest_sums[last * width :][:1] + wide(first_got[width:])
        half = spans // 2
        while half > 1:
            got = swap(total[half - 1 :], half << near)
            total = total[: half - 1] + wide(got[1:])
            among.append(got[:1])
            half = half // 2
        across = swap(total, 1 << near)
        early = pl.pallas_call(
            early_kernel,
            out_shape=jax.ShapeDtypeStruct((per_core, 2 * modes, pairs), jnp.float32),
            in_specs=[vmem] * (2 + len(among)),
            out_specs=vmem,
            compiler_params=pltpu.CompilerParams(vmem_limit_bytes=4 * 2**20),
            cost_estimate=pl.CostEstimate(
                flops=2 * mixer.size * per_core * pairs, bytes_accessed=16 * per_core * modes * pairs, transcendentals=0
            ),
            name="rotate_early",
        )(mixer, own, *among)
        return pl.pallas_call(
            late_kernel,
            out_shape=jax.ShapeDtypeStruct((1, 2, per_core, modes, pairs), jnp.bfloat16),
            in_specs=[vmem] * 3,
            out_specs=vmem,
            compiler_params=pltpu.CompilerParams(vmem_limit_bytes=4 * 2**20),
            name="rotate_last",
        )(mixer, early, across)

    return shards


def solution(mesh):
    return jax.shard_map(
        make_shards(mesh),
        mesh=mesh,
        in_specs=(
            P(None, "rp", "re", None, None),
            P(None, "rp"),
            P(),
            P(None, "grp"),
            P(None, "grp"),
            P(("grp", "rp"), None, None, None),
        ),
        out_specs=P(("grp", "rp"), None, "re", None, None),
        check_vma=False,
    )
```

```python
import math

import jax
import jax.numpy as jnp
from jax import lax
from jax.experimental import pallas as pl
from jax.experimental.pallas import tpu as pltpu
from jax.sharding import PartitionSpec as P

NFINE = 48
NEAR = 2
PIECES = 4
ROWS = 16


def near_bits(bits):
    return min(NEAR, bits - 1)


def slot_offsets(bits):
    near = near_bits(bits)
    last = (1 << near) - 1
    beyond = [f << near for f in range(1, 1 << (bits - near))]
    return [last | far for far in (*beyond, 0)], [d | far for d in range(last) for far in beyond] + list(range(last))


def wrapped_angle(products):
    turns = jnp.floor((products + 0.5) * (1.0 / NFINE))
    return (products - NFINE * turns) * (2.0 * math.pi / NFINE)


def k_phases(core, per_core, slab, k_ref, ev_ref):
    places = (2 * per_core, slab)
    at_row = lax.broadcasted_iota(jnp.int32, places, 0)
    at_lane = lax.broadcasted_iota(jnp.int32, places, 1)
    products = jnp.zeros(places, jnp.float32)
    for line in range(2 * per_core):
        k = (core ^ (line // per_core)) * per_core + line % per_core
        for e in range(slab):
            total = 0
            for axis in range(3):
                total = total + k_ref[k, axis] * ev_ref[axis, core * slab + e]
            products = jnp.where((at_row == line) & (at_lane == e), total.astype(jnp.float32), products)
    angles = wrapped_angle(products)
    return jnp.cos(angles), jnp.sin(angles)


def k_sum(prod_ref, c, slot, k_cos, k_sin, line):
    slab, _, pairs = prod_ref.shape[1:]
    real = imag = None
    for e in range(slab):
        p_real = prod_ref[c, e, pl.ds(2 * slot * ROWS, ROWS), :]
        p_imag = prod_ref[c, e, pl.ds((2 * slot + 1) * ROWS, ROWS), :]
        cos_e = jnp.broadcast_to(k_cos[line : line + 1, e : e + 1], (ROWS, pairs))
        sin_e = jnp.broadcast_to(k_sin[line : line + 1, e : e + 1], (ROWS, pairs))
        r_term = cos_e * p_real - sin_e * p_imag
        i_term = sin_e * p_real + cos_e * p_imag
        real = r_term if e == 0 else real + r_term
        imag = i_term if e == 0 else imag + i_term
    return real, imag


def phase_kernel(bits, q_hbm, k_hbm, ev_hbm, rpv_hbm, eig_hbm, w_ref, prod_ref, first_ref, rest_ref, turn_ref, mixer_ref,
                 slabs, lhs, rpv_ref, eig_ref, q_ref, k_ref, ev_ref, sems, small_sems):
    parts, points, slab, modes, pairs = w_ref.shape
    first_slots, per_core = first_ref.shape[:2]
    slots = first_slots + rest_ref.shape[0]
    chunks = modes // ROWS
    pieces = sems.shape[1]

    small = [
        pltpu.make_async_copy(source, target, small_sems.at[at])
        for at, (source, target) in enumerate(
            [(rpv_hbm, rpv_ref), (q_hbm, q_ref), (k_hbm, k_ref), (ev_hbm, ev_ref), (eig_hbm, eig_ref)]
        )
    ]
    for copy in small:
        copy.start()

    def fetch(c, piece):
        some = pl.ds(piece * (points // pieces), points // pieces)
        return pltpu.make_async_copy(
            w_ref.at[:, some, :, pl.ds(c * ROWS, ROWS), :], slabs.at[c, :, some], sems.at[c, piece]
        )

    for c in range(chunks):
        for piece in range(pieces):
            fetch(c, piece).start()
    for copy in small:
        copy.wait()

    me = lax.axis_index("rp")
    core = lax.axis_index("re")
    width = points * ROWS
    spread = (
        lax.broadcasted_iota(jnp.int32, (points, width), 1) // ROWS
        == lax.broadcasted_iota(jnp.int32, (points, width), 0)
    ).astype(jnp.bfloat16)
    vectors = jnp.dot(rpv_ref[...].astype(jnp.bfloat16), spread, preferred_element_type=jnp.float32)
    rows = []
    for offset in sum(slot_offsets(bits), []):
        q = me ^ offset
        row = 0.0
        for axis in range(3):
            row = row + q_ref[axis, q].astype(jnp.float32) * vectors[axis : axis + 1, :]
        rows.append(row)
    angles = wrapped_angle(jnp.concatenate(rows, axis=0))
    cosine, sine = jnp.cos(angles), jnp.sin(angles)
    diagonal = (
        lax.broadcasted_iota(jnp.int32, (ROWS, width), 1) % ROWS
        == lax.broadcasted_iota(jnp.int32, (ROWS, width), 0)
    ).astype(jnp.float32)
    for slot in range(slots):
        cos_block = (cosine[slot : slot + 1] * diagonal).astype(jnp.bfloat16)
        sin_block = (sine[slot : slot + 1] * diagonal).astype(jnp.bfloat16)
        top, bottom = pl.ds(2 * slot * ROWS, ROWS), pl.ds((2 * slot + 1) * ROWS, ROWS)
        lhs[top, :width] = cos_block
        lhs[top, width:] = -sin_block
        lhs[bottom, :width] = sin_block
        lhs[bottom, width:] = cos_block

    k_cos, k_sin = k_phases(core, per_core, slab, k_ref, ev_ref)
    turn_ref[0] = k_cos
    turn_ref[1] = k_sin

    real_vec, imag_vec = eig_ref[0, 0], eig_ref[0, 1]
    rotation = jnp.concatenate(
        [jnp.concatenate([real_vec, imag_vec], axis=1), jnp.concatenate([-imag_vec, real_vec], axis=1)], axis=0
    )
    turned = rotation.T
    high = turned.astype(jnp.bfloat16)
    low = (turned - high.astype(jnp.float32)).astype(jnp.bfloat16)
    mixer_ref[...] = jnp.concatenate([high, low, high], axis=1)

    def send_sum(c):
        for slot in range(slots):
            for i in range(per_core):
                sums = k_sum(prod_ref, c, slot, k_cos, k_sin, per_core + i)
                for part in range(2):
                    place = (i, part, pl.ds(c * ROWS, ROWS), slice(None))
                    if slot < first_slots:
                        first_ref[(slot, *place)] = sums[part].astype(first_ref.dtype)
                    else:
                        rest_ref[(slot - first_slots, *place)] = sums[part].astype(rest_ref.dtype)

    for c in range(chunks):
        if c:
            send_sum(c - 1)
        for piece in range(pieces):
            fetch(c, piece).wait()
        for e in range(slab):
            block = slabs[c, :, :, e].reshape(parts * width, pairs)
            prod_ref[c, e] = jnp.dot(lhs[...], block, preferred_element_type=jnp.float32)
    send_sum(chunks - 1)


def keep_kernel(prod_ref, turn_ref, first_ref, rest_ref):
    first_slots, per_core = first_ref.shape[:2]
    slots = first_slots + rest_ref.shape[0]
    k_cos, k_sin = turn_ref[0], turn_ref[1]
    for c in range(prod_ref.shape[0]):
        for slot in range(slots):
            for i in range(per_core):
                sums = k_sum(prod_ref, c, slot, k_cos, k_sin, i)
                for part in range(2):
                    place = (i, part, pl.ds(c * ROWS, ROWS), slice(None))
                    if slot < first_slots:
                        first_ref[(slot, *place)] = sums[part]
                    else:
                        rest_ref[(slot - first_slots, *place)] = sums[part]


def early_kernel(mixer_ref, mine_ref, *refs):
    *got_refs, out_ref = refs
    modes, pairs = mine_ref.shape[-2:]
    mixer = mixer_ref[...]
    for i in range(mine_ref.shape[1]):
        source = mine_ref[0, i]
        for got_ref in got_refs:
            source = source + got_ref[0, i].astype(jnp.float32)
        source = source.reshape(2 * modes, pairs)
        high = source.astype(jnp.bfloat16)
        low = (source - high.astype(jnp.float32)).astype(jnp.bfloat16)
        stacked = jnp.concatenate([high, high, low], axis=0)
        out_ref[i] = jnp.dot(mixer, stacked, preferred_element_type=jnp.float32)


def late_kernel(mixer_ref, early_ref, got_ref, out_ref):
    modes, pairs = got_ref.shape[-2:]
    mixer = mixer_ref[:, : 4 * modes]
    for i in range(got_ref.shape[1]):
        got = got_ref[0, i].reshape(2 * modes, pairs)
        turned = jnp.dot(mixer, jnp.concatenate([got, got], axis=0), preferred_element_type=jnp.float32)
        turned = (early_ref[i] + turned).astype(out_ref.dtype)
        out_ref[0, 0, i] = turned[:modes]
        out_ref[0, 1, i] = turned[modes:]


def make_shards(mesh):
    ranks, cores = mesh.shape["rp"], mesh.shape["re"]
    bits = ranks.bit_length() - 1
    vmem = pl.BlockSpec(memory_space=pltpu.VMEM)
    hbm = pl.BlockSpec(memory_space=pltpu.HBM)

    def in_hbm(x):
        return pltpu.with_memory_space_constraint(x, pltpu.HBM)

    def shards(weights, rp_vectors, re_vectors, q_points, k_points, eigvecs):
        parts, points, slab, modes, pairs = weights.shape
        slots = q_points.shape[1]
        per_core = k_points.shape[1] // cores
        chunks = modes // ROWS
        near = near_bits(bits)
        groups, spans = 1 << near, 1 << (bits - near)
        block = (per_core, 2, modes, pairs)
        shapes = [(spans, *block), (slots - spans, *block)]
        pieces = math.gcd(points, PIECES)
        lines = 2 * slots * ROWS
        prod, first_away, rest_away, turn, mixer = pl.pallas_call(
            lambda *refs: phase_kernel(bits, *refs),
            out_shape=(
                jax.ShapeDtypeStruct((chunks, slab, lines, pairs), jnp.float32),
                *[jax.ShapeDtypeStruct(shape, jnp.bfloat16) for shape in shapes],
                jax.ShapeDtypeStruct((2, 2 * per_core, slab), jnp.float32),
                jax.ShapeDtypeStruct((2 * modes, 6 * modes), jnp.bfloat16),
            ),
            in_specs=[hbm] * 6,
            out_specs=(vmem,) * 5,
            scratch_shapes=[
                pltpu.VMEM((chunks, parts, points, slab, ROWS, pairs), jnp.bfloat16),
                pltpu.VMEM((lines, parts * points * ROWS), jnp.bfloat16),
                pltpu.VMEM(rp_vectors.shape, jnp.int32),
                pltpu.VMEM(eigvecs.shape, jnp.float32),
                pltpu.SMEM(q_points.shape, jnp.int32),
                pltpu.SMEM(k_points.shape[::-1], jnp.int32),
                pltpu.SMEM(re_vectors.shape, jnp.int32),
                pltpu.SemaphoreType.DMA((chunks, pieces)),
                pltpu.SemaphoreType.DMA((5,)),
            ],
            compiler_params=pltpu.CompilerParams(vmem_limit_bytes=16 * 2**20),
            name="phase_sums",
        )(*[in_hbm(x) for x in (q_points, k_points.T, re_vectors, rp_vectors, eigvecs, weights)])
        first_sums, rest_sums = pl.pallas_call(
            keep_kernel,
            out_shape=[jax.ShapeDtypeStruct(shape, jnp.float32) for shape in shapes],
            in_specs=[vmem, vmem],
            out_specs=[vmem, vmem],
            compiler_params=pltpu.CompilerParams(vmem_limit_bytes=4 * 2**20),
            cost_estimate=pl.CostEstimate(flops=8 * prod.size, bytes_accessed=4 * prod.size, transcendentals=0),
            name="own_k_sums",
        )(prod, turn)

        def swap(blocks, offset, axis="rp"):
            size = mesh.shape[axis]
            ends = [(r, r ^ offset) for r in range(size)]
            return lax.ppermute(blocks.astype(jnp.bfloat16), axis, ends)

        def wide(blocks):
            return blocks.astype(jnp.float32)

        first_other = swap(first_away, 1, "re")
        rest_other = swap(rest_away, 1, "re")
        last = groups - 1
        first_sums = first_sums + wide(first_other)
        rest_sums = rest_sums + wide(rest_other)
        first_got = swap(first_sums, last)
        width = spans - 1
        beyond = [swap(rest_sums[d * width : (d + 1) * width], d) for d in reversed(range(1, last))]
        among = [swap(rest_sums[last * width + d :][:1], d) for d in reversed(range(1, last))]
        total = rest_sums[:width] + wide(first_got[:width])
        for got in beyond:
            total = total + wide(got)
        own = rest_sums[last * width :][:1] + wide(first_got[width:])
        half = spans // 2
        while half > 1:
            got = swap(total[half - 1 :], half << near)
            total = total[: half - 1] + wide(got[1:])
            among.append(got[:1])
            half = half // 2
        across = swap(total, 1 << near)
        early = pl.pallas_call(
            early_kernel,
            out_shape=jax.ShapeDtypeStruct((per_core, 2 * modes, pairs), jnp.float32),
            in_specs=[vmem] * (2 + len(among)),
            out_specs=vmem,
            compiler_params=pltpu.CompilerParams(vmem_limit_bytes=4 * 2**20),
            cost_estimate=pl.CostEstimate(
                flops=2 * mixer.size * per_core * pairs, bytes_accessed=16 * per_core * modes * pairs, transcendentals=0
            ),
            name="rotate_early",
        )(mixer, own, *among)
        return pl.pallas_call(
            late_kernel,
            out_shape=jax.ShapeDtypeStruct((1, 2, per_core, modes, pairs), jnp.bfloat16),
            in_specs=[vmem] * 3,
            out_specs=vmem,
            compiler_params=pltpu.CompilerParams(vmem_limit_bytes=4 * 2**20),
            name="rotate_last",
        )(mixer, early, across)

    return shards


def solution(mesh):
    return jax.shard_map(
        make_shards(mesh),
        mesh=mesh,
        in_specs=(
            P(None, "rp", "re", None, None),
            P(None, "rp"),
            P(),
            P(None, "grp"),
            P(None, "grp"),
            P(("grp", "rp"), None, None, None),
        ),
        out_specs=P(("grp", "rp"), None, "re", None, None),
        check_vma=False,
    )
```
